32 devices in a mesh: angle: 8 (over y, x, core), frame: 4 (over z).
Axes of the slice: x: 2, y: 2, z: 4, core: 2. Of those that a mesh axis runs over, the one named last changes fastest.
Arguments:
- volume: float32 [32, 8192], P('frame', 'angle'), may hold values from -6 to 6
- measured: bfloat16 [8, 32, 12288], P(None, 'frame', 'angle'), may hold values from -6 to 6
- tiles: bfloat16 [8, 1024, 1536], replicated, may hold values from -0.0625 to 0.0625
- tile_index: int32 [8, 8], replicated, may hold values from 0 to 7, as said below
- warp_coef: bfloat16 [8, 3, 32, 8192], P(None, None, 'frame', 'angle'), may hold values from 0.099609375 to 0.59765625
- warp_offset: int32 [8, 32], P(None, 'frame'), may hold values from -2 to 0
- ray_weight: float32 [32, 12288], P('frame', 'angle'), may hold values from 0.5 to 2
- redundancy: float32 [12288], P('angle'), may hold values from 0.2 to 0.8
- conj_view: int32 [8, 2], P('angle'), may hold values from 0 to 1, as said below
- voxel_weight: float32 [32, 8192], P('frame', 'angle'), may hold values from 0.05 to 0.2
Outputs:
- volume_next: float32 [32, 8192], P('frame', 'angle')
- weighted: bfloat16 [8, 32, 12288], P(None, 'frame', 'angle')
The draws below stay inside these ranges and needn't reach their ends.
Inputs may be any that keep to these rules, and one draw needn't show every extreme that they name: `conj_view`: each row is a permutation of 0..1, and row b + 4 is the inverse permutation of row b for b < 4. `tile_index`: every row is a permutation of 0..7.
All inputs are finite; a program needn't handle non-finite values.
Results may differ from the reference program's by a relative error of at most 0.0034.
Values may be sent and summed in bfloat16 or wider, within the bound.
A program may use at most 256 MiB of HBM per device.

```python
import math
import jax
import jax.numpy as jnp
from jax import lax

F = 8
VS = 1024
VB = 2
UW = 768
TAPS = 3
HALO = 2
Z = 32
BLOCKS = 8
TB = 8
V = 8192
P_SIZE = 1536
RAYS = 12288


def draw_conj_view(key, part):
    half_count = BLOCKS // 2
    keys = jax.random.split(key, half_count)
    onward = jax.vmap(lambda one_key: jax.random.permutation(one_key, VB))(keys).astype(jnp.int32)
    inverse = jnp.argsort(onward, axis=1).astype(jnp.int32)
    return jnp.concatenate([onward, inverse], axis=0)


def draw_tile_index(key, part):
    row_keys = jax.random.split(jax.random.fold_in(key, 7), BLOCKS)
    rows = jax.vmap(lambda one_key: jax.random.permutation(one_key, TB))(row_keys)
    return rows.astype(jnp.int32)


def place_ends(entries, own_key, smallest, high):
    shape = entries.shape
    index_at = [jax.random.randint(jax.random.fold_in(own_key, axis), (), 0, shape[axis]) for axis in range(len(shape))]
    entries = entries.at[tuple(index_at)].set(smallest)
    longest = shape.index(max(shape))
    index_at[longest] = (index_at[longest] + 1) % shape[longest]
    return entries.at[tuple(index_at)].set(high)


def block_levels(stream_key, extent, cuts, smallest, largest):
    gain = 1.0
    for dim, parts in cuts:
        steps = jax.random.uniform(jax.random.fold_in(jax.random.fold_in(stream_key, 6), dim), (parts,), jnp.float32, smallest / len(cuts), largest / len(cuts))
        gain = gain * jnp.repeat(jnp.exp(steps), extent[dim] // parts).reshape((-1,) + (1,) * (len(extent) - 1 - dim))
    return gain


def normal_values(rng, shape, deviation, limit, cuts=(), held_as=jnp.bfloat16):
    result = jax.random.normal(rng, shape, jnp.float32) * deviation
    if len(cuts) > 0:
        result = block_levels(rng, shape, cuts, -0.22, 0.18) * result
    return jnp.clip(result, min=-limit, max=limit).astype(held_as)


def setup_inputs(seed: int = 0) -> dict:
    key_list = jax.random.split(jax.random.key(seed), 11)
    return {
        "volume": normal_values(key_list[0], (Z, V), 1.0, 6.0, ((0, 4), (1, 8)), jnp.float32),
        "measured": normal_values(key_list[1], (F, Z, RAYS), 1.0, 6.0, ((1, 4), (2, 8))),
        "tiles": normal_values(key_list[2], (TB, VS, P_SIZE), V ** -0.5, 0.0625),
        "tile_index": draw_tile_index(jax.random.fold_in(key_list[10], 71), 0),
        "warp_coef": jnp.clip(0.099609375 + 0.49804688 * jax.random.uniform(key_list[4], (F, TAPS, Z, V), jnp.float32) ** block_levels(key_list[4], (F, TAPS, Z, V), ((2, 4), (3, 8)), -0.2, 0.2), 0.099609375, 0.59765625).astype(jnp.bfloat16),
        "warp_offset": place_ends(jax.random.randint(key_list[5], (F, Z), 0 - HALO, 1), jax.random.fold_in(key_list[5], 1), 0 - HALO, 0).astype(jnp.int32),
        "ray_weight": jnp.clip(jnp.exp(math.log(2.0) - 1.3862944 * jax.random.uniform(key_list[6], (Z, RAYS), jnp.float32) ** block_levels(key_list[6], (Z, RAYS), ((0, 4), (1, 8)), -0.2, 0.2)), 0.5, 2.0),
        "redundancy": jnp.clip(0.2 + 0.6 * jax.random.uniform(key_list[7], (RAYS,), jnp.float32) ** block_levels(key_list[7], (RAYS,), ((0, 8),), -0.2, 0.2), 0.2, 0.8),
        "conj_view": draw_conj_view(jax.random.fold_in(key_list[10], 71), 0),
        "voxel_weight": jnp.clip(jnp.exp(math.log(0.2) - 1.3862944 * jax.random.uniform(key_list[9], (Z, V), jnp.float32) ** block_levels(key_list[9], (Z, V), ((0, 4), (1, 8)), -0.2, 0.2)), 0.05, 0.2),
    }


def warp_weights(offsets, coefs, distance):
    weights = jnp.zeros(coefs[:, 0].shape, jnp.float32)
    for tap_index in range(coefs.shape[1]):
        selected = (offsets + tap_index == distance).astype(jnp.float32)[:, :, None]
        weights = weights + selected * coefs[:, tap_index].astype(jnp.float32)
    return weights


def reference(volume, measured, tiles, tile_index, warp_coef, warp_offset, ray_weight, redundancy, conj_view, voxel_weight):
    padded = jnp.pad(volume, ((HALO, HALO), (0, 0)))
    warped = jnp.zeros((F, Z, V), jnp.float32)
    for distance in range(-HALO, HALO + 1):
        source_rows = padded[HALO + distance:HALO + distance + Z]
        warped = warped + warp_weights(warp_offset, warp_coef, distance) * source_rows[None]
    stacked_rows = warped.astype(jnp.bfloat16).reshape(F * Z, V)

    def project_block(block):
        def add_sector(sector_no, running):
            part = lax.dynamic_slice_in_dim(stacked_rows, sector_no * VS, VS, 1)
            footprint = tiles[tile_index[block, sector_no]]
            return running + jnp.dot(part, footprint, preferred_element_type=jnp.float32)
        return lax.fori_loop(0, BLOCKS, add_sector, jnp.zeros((F * Z, P_SIZE), jnp.float32))

    projected = lax.map(project_block, jnp.arange(BLOCKS, dtype=jnp.int32))
    projected = projected.reshape(BLOCKS, F, Z, P_SIZE).transpose(1, 2, 0, 3).reshape(F, Z, RAYS)
    residual = measured.astype(jnp.float32) - projected
    block_view = residual.reshape(F, Z, BLOCKS, VB, UW)
    partner = jnp.roll(block_view, -(BLOCKS // 2), axis=2)
    picks = jnp.broadcast_to(conj_view[None, None, :, :, None], (F, Z, BLOCKS, VB, UW))
    mirrored = jnp.take_along_axis(partner, picks, axis=3)[..., ::-1].reshape(F, Z, RAYS)
    weighted = ((redundancy * residual + (1.0 - redundancy) * mirrored) * ray_weight[None]).astype(jnp.bfloat16)
    ray_rows = weighted.reshape(F * Z, RAYS)

    def back_sector(sector_no):
        def add_block(block, running):
            part = lax.dynamic_slice_in_dim(ray_rows, block * P_SIZE, P_SIZE, 1)
            footprint = tiles[tile_index[block, sector_no]]
            return running + lax.dot_general(part, footprint, (((1,), (1,)), ((), ())), preferred_element_type=jnp.float32)
        return lax.fori_loop(0, BLOCKS, add_block, jnp.zeros((F * Z, VS), jnp.float32))

    images = lax.map(back_sector, jnp.arange(BLOCKS, dtype=jnp.int32))
    images = images.transpose(1, 0, 2).reshape(F, Z, V)
    gathered = jnp.zeros((Z, V), jnp.float32)
    for distance in range(-HALO, HALO + 1):
        terms = jnp.sum(warp_weights(warp_offset, warp_coef, distance) * images, axis=0)
        padded_terms = jnp.pad(terms, ((HALO, HALO), (0, 0)))
        gathered = gathered + padded_terms[HALO - distance:HALO - distance + Z]
    return volume + voxel_weight * gathered, weighted
```

```python
import functools

import jax
import jax.numpy as jnp
from jax import lax
from jax.experimental import pallas as pl
from jax.experimental.pallas import tpu as pltpu
from jax.sharding import PartitionSpec as P

VB = 2
HALO = 2
TAPS = 3
MESH = pl.DeviceIdType.MESH
F32 = jnp.float32
BF16 = jnp.bfloat16


def kernel(
    blocks,
    slabs,
    frames,
    rows,
    volume_hbm,
    measured_hbm,
    tiles_hbm,
    index_hbm,
    coefs_hbm,
    offsets_hbm,
    weight_hbm,
    red_hbm,
    conj_hbm,
    voxel_hbm,
    next_hbm,
    weighted_hbm,
    volume,
    measured,
    coefs,
    offsets,
    ray_weight,
    redundancy,
    voxel_weight,
    tile_index,
    conj_view,
    find,
    next_ref,
    tiles,
    gathered,
    away,
    proj_mine,
    proj_out,
    proj_in,
    part_measured,
    part_weight,
    part_red,
    wall,
    wall_in,
    product,
    image,
    vol_out,
    vol_in,
    adj_out,
    adj_in,
    sib_out,
    sib_in,
    far_out,
    far_in,
    in_sem,
    out_sem,
    tile_sem,
    ag_send,
    ag_recv,
    fw_send,
    fw_recv,
    pt_send,
    pt_recv,
    pj_send,
    pj_recv,
    wt_send,
    wt_recv,
    hv_send,
    hv_recv,
    ha_send,
    ha_recv,
    sb_send,
    sb_recv,
    fr_send,
    fr_recv,
):
    me = lax.axis_index("angle")
    slab = lax.axis_index("frame")
    chips = blocks // 2
    ring = chips // 2
    core = lax.rem(me, 2)
    chip = me // 2
    half = chip // ring
    place = lax.rem(chip, ring)
    sibling = me + 1 - 2 * core

    def chip_at(dh, dp):
        return lax.rem(half + dh, 2) * ring + lax.rem(place + dp, ring)

    def chip_from(dh, dp):
        return lax.rem(half + dh, 2) * ring + lax.rem(place + ring - dp, ring)

    partner = 2 * chip_at(1, 0) + core
    group = [me, partner, sibling, 2 * chip_at(1, 0) + 1 - core]
    others = [(dh, dp) for dp in range(ring) for dh in range(2) if dh or dp]
    everyone = [(0, 0)] + others
    count = tiles.shape[0]
    first = core * count
    stacked = frames * rows // 2
    sector = volume.shape[1]
    rays = measured.shape[1]
    view = rays // VB
    has_low = slab > 0
    has_high = slab < slabs - 1

    def remote(src, dst, send, recv, angle, frame=slab):
        return pltpu.make_async_remote_copy(
            src_ref=src,
            dst_ref=dst,
            send_sem=send,
            recv_sem=recv,
            device_id=(angle, frame),
            device_id_type=MESH,
        )

    def tile_copy(t):
        return pltpu.make_async_copy(tiles_hbm.at[first + t], tiles.at[t], tile_sem.at[t])

    barrier = pltpu.get_barrier_semaphore()
    pl.semaphore_signal(barrier, inc=1, device_id=(sibling, slab), device_id_type=MESH)
    for dh, dp in others:
        pl.semaphore_signal(
            barrier, inc=1, device_id=(2 * chip_at(dh, dp) + core, slab), device_id_type=MESH
        )

    @pl.when(has_low)
    def _():
        pl.semaphore_signal(barrier, inc=1, device_id=(me, slab - 1), device_id_type=MESH)

    @pl.when(has_high)
    def _():
        pl.semaphore_signal(barrier, inc=1, device_id=(me, slab + 1), device_id_type=MESH)

    measured_half = measured_hbm.at[pl.ds(pl.multiple_of(half * stacked, 16), stacked)]
    measured_away = measured_hbm.at[pl.ds(pl.multiple_of((1 - half) * stacked, 16), stacked)]
    local = [
        pltpu.make_async_copy(src, dst, in_sem.at[n])
        for n, (src, dst) in enumerate(
            (
                (volume_hbm, volume),
                (coefs_hbm, coefs),
                (offsets_hbm, offsets),
                (index_hbm, tile_index),
                (conj_hbm, conj_view),
                (measured_half, measured),
                (weight_hbm, ray_weight),
                (red_hbm, redundancy),
                (voxel_hbm, voxel_weight),
            )
        )
    ]
    for copy in local:
        copy.start()
    local[0].wait()
    vol = volume[...]
    vol_out[0] = vol[:HALO]
    vol_out[1] = vol[rows - HALO :]

    peers = chips + has_low.astype(jnp.int32) + has_high.astype(jnp.int32)
    pl.semaphore_wait(barrier, peers)

    def halo(out, into, send, recv, side):
        return remote(
            out.at[side], into.at[1 - side], send.at[side], recv.at[1 - side], me, slab + 2 * side - 1
        )

    def exchange(out, into, send, recv):
        @pl.when(has_low)
        def _():
            halo(out, into, send, recv, 0).start()

        @pl.when(has_high)
        def _():
            halo(out, into, send, recv, 1).start()

    def exchange_wait(out, into, send, recv):
        @pl.when(has_low)
        def _():
            halo(out, into, send, recv, 0).wait_send()
            halo(out, into, send, recv, 1).wait_recv()

        @pl.when(has_high)
        def _():
            halo(out, into, send, recv, 1).wait_send()
            halo(out, into, send, recv, 0).wait_recv()

        @pl.when(slab == 0)
        def _():
            into[0] = jnp.zeros_like(into[0])

        @pl.when(slab == slabs - 1)
        def _():
            into[1] = jnp.zeros_like(into[1])

    exchange(vol_out, vol_in, hv_send, hv_recv)
    local[1].wait()
    local[2].wait()

    off = offsets[...].astype(F32)
    lane = lax.broadcasted_iota(jnp.int32, (rows, rows), 1)
    diagonal = lane == lax.broadcasted_iota(jnp.int32, (rows, rows), 0)

    def offset_column(f):
        spread = jnp.broadcast_to(off[f : f + 1, :], (rows, rows))
        return jnp.sum(jnp.where(diagonal, spread, 0.0), axis=1, keepdims=True)

    columns = [offset_column(f) for f in range(frames)]
    pair = 2 * TAPS * rows

    def warp(below, above):
        extended = jnp.concatenate([below, vol, above], axis=0)
        sources = [extended[m : m + rows] for m in range(2 * HALO + 1)]
        warped = []
        for p in range(frames // 2):
            taps = coefs[p * pair : (p + 1) * pair, :].astype(F32)
            for i in range(2):
                column = columns[2 * p + i]
                low = column == -2.0
                mid = column == -1.0
                total = None
                for k in range(TAPS):
                    start = (i * TAPS + k) * rows
                    chosen = jnp.where(
                        low, sources[k], jnp.where(mid, sources[k + 1], sources[k + 2])
                    )
                    term = taps[start : start + rows] * chosen
                    total = term if total is None else total + term
                warped.append(total)
        return warped

    def keep(j, pieces):
        each = len(pieces) // 2
        early = jnp.concatenate(pieces[:each], axis=0)
        late = jnp.concatenate(pieces[each:], axis=0)
        gathered[me, j] = jnp.where(half == 0, early, late).astype(BF16)
        away[j] = jnp.where(half == 0, late, early).astype(BF16)

    def slot(dh, dp):
        return dh * ring + dp

    def cross(dh, dp, j):
        return remote(
            away.at[j] if dh else gathered.at[me, j],
            gathered.at[me, j],
            ag_send.at[slot(dh, dp), j],
            ag_recv.at[slot(dh, dp), j],
            2 * chip_at(dh, dp) + core,
        )

    def to_sibling(dh, dp, j):
        block = 2 * chip_from(dh, dp) + core
        return remote(
            gathered.at[block, j],
            gathered.at[block, j],
            fw_send.at[slot(dh, dp), j],
            fw_recv.at[slot(dh, dp), j],
            sibling,
        )

    def spread_chunk(j):
        for dh, dp in reversed(others):
            cross(dh, dp, j).start()
        to_sibling(0, 0, j).start()

    def pass_chunk(j):
        for dh, dp in others:
            cross(dh, dp, j).wait_recv()
            to_sibling(dh, dp, j).start()

    partner_copies = [
        remote(measured_away, part_measured, pt_send.at[0], pt_recv.at[0], partner),
        remote(weight_hbm, part_weight, pt_send.at[1], pt_recv.at[1], partner),
        remote(red_hbm, part_red, pt_send.at[2], pt_recv.at[2], partner),
    ]
    outside = jnp.zeros((HALO, sector), F32)
    keep(0, [value[HALO : rows - HALO] for value in warp(outside, outside)])
    spread_chunk(0)
    for t in range(count):
        tile_copy(t).start()
    for copy in partner_copies[1:]:
        copy.start()
    exchange_wait(vol_out, vol_in, hv_send, hv_recv)
    outer = []
    for value in warp(vol_in[0], vol_in[1]):
        outer += [jnp.concatenate([value[:HALO], value[rows - HALO :]], axis=0)]
    keep(1, outer)
    spread_chunk(1)
    partner_copies[0].start()

    local[3].wait()
    for q in range(4):
        row = [tile_index[group[q], s] for s in range(blocks)]
        for t in range(count):
            at = jnp.int32(0)
            for s in range(blocks):
                at = jnp.where(row[s] == first + t, s, at)
            find[q, t] = at

    pass_chunk(0)
    pass_chunk(1)
    for t in range(count):
        tile_copy(t).wait()
    for j in range(2):
        for dh, dp in everyone:
            to_sibling(dh, dp, j).wait_recv()

    wide = 256
    parts = rays // wide
    each = view // wide

    def proj_copy(n):
        return remote(proj_out.at[n], proj_in.at[n], pj_send.at[n], pj_recv.at[n], sibling)

    for n in range(parts):
        total = None
        for t in range(count):
            left = jnp.concatenate(
                [gathered[find[q, t]].reshape(stacked, sector) for q in range(4)], axis=0
            )
            term = jnp.dot(
                left, tiles[t, :, n * wide : (n + 1) * wide], preferred_element_type=F32
            )
            total = term if total is None else total + term
        proj_mine[n] = total[: 2 * stacked]
        proj_out[n] = total[2 * stacked :]
        proj_copy(n).start()

    for copy in local[4:]:
        copy.wait()
    for copy in partner_copies:
        copy.wait_recv()

    inside = rows - 2 * HALO
    chunk = frames * inside // 2

    def in_order(value, base):
        pieces = []
        for f in range(frames // 2):
            a = base + f * inside
            b = base + chunk + f * 2 * HALO
            pieces += [value[b : b + HALO], value[a : a + inside], value[b + HALO : b + 2 * HALO]]
        return jnp.concatenate(pieces, axis=0)

    flip = lax.broadcasted_iota(jnp.int32, (wide, wide), 0) + lax.broadcasted_iota(
        jnp.int32, (wide, wide), 1
    )
    flip = jnp.where(flip == wide - 1, 1.0, 0.0).astype(BF16)
    swap = conj_view[0, 0] == 1
    residuals = []
    flipped = []
    for n in range(parts):
        span = slice(n * wide, (n + 1) * wide)
        proj_copy(n).wait_recv()
        value = proj_mine[n] + proj_in[n]
        value = jnp.concatenate(
            [
                measured[:, span].astype(F32) - in_order(value, 0),
                part_measured[:, span].astype(F32) - in_order(value, stacked),
            ],
            axis=0,
        )
        high = value.astype(BF16)
        rest = (value - high.astype(F32)).astype(BF16)
        residuals.append(value)
        flipped.append(
            jnp.dot(high, flip, preferred_element_type=F32)
            + jnp.dot(rest, flip, preferred_element_type=F32)
        )

    def combine(residual, mirrored, red, weight):
        red = jnp.broadcast_to(red, residual.shape)
        value = red * residual + (1.0 - red) * mirrored
        return (value * jnp.concatenate([weight] * (frames // 2), axis=0)).astype(BF16)

    red_own = redundancy[...][None, :]
    red_part = part_red[...][None, :]
    for w in range(VB):
        for u in range(each):
            n = w * each + u
            span = slice(n * wide, (n + 1) * wide)
            straight = flipped[w * each + each - 1 - u]
            crossed = flipped[(VB - 1 - w) * each + each - 1 - u]
            mirrored = jnp.where(swap, crossed, straight)
            wall[:stacked, span] = combine(
                residuals[n][:stacked], mirrored[stacked:], red_own[:, span], ray_weight[:, span]
            )
            wall[stacked:, span] = combine(
                residuals[n][stacked:], mirrored[:stacked], red_part[:, span], part_weight[:, span]
            )

    wall_copy = remote(wall, wall_in, wt_send.at[0], wt_recv.at[0], sibling)
    wall_copy.start()
    place_rows = pl.ds(pl.multiple_of(half * stacked, 16), stacked)
    out_weighted = pltpu.make_async_copy(
        wall.at[pl.ds(0, stacked)], weighted_hbm.at[place_rows], out_sem.at[0]
    )
    out_weighted.start()
    back_copy = remote(
        wall.at[pl.ds(stacked, stacked)],
        weighted_hbm.at[place_rows],
        wt_send.at[1],
        wt_recv.at[1],
        partner,
    )
    back_copy.start()
    wall_copy.wait_recv()

    cuts = 2
    width = sector // cuts

    def multiply(c):
        both = jnp.concatenate([wall[...], wall_in[...]], axis=0)
        for t in range(count):
            product[c, t] = lax.dot_general(
                both,
                tiles[t, c * width : (c + 1) * width, :],
                (((1,), (1,)), ((), ())),
                preferred_element_type=F32,
            )

    def partial(c, s):
        total = None
        for q in range(4):
            t = tile_index[group[q], s] - first
            ours = jnp.logical_and(t >= 0, t < count)
            t = jnp.where(ours, t, 0)
            term = jnp.where(ours, product[c, t, q * stacked : (q + 1) * stacked, :], 0.0)
            total = term if total is None else total + term
        return total

    def sib_copy(c):
        return remote(sib_out.at[c], sib_in.at[c], sb_send.at[c], sb_recv.at[c], sibling)

    def far_copy(c, dh, dp):
        i = slot(dh, dp)
        return remote(
            far_out.at[c, i],
            far_in.at[c, i],
            fr_send.at[c, i],
            fr_recv.at[c, i],
            2 * chip_at(dh, dp) + core,
        )

    def give(c):
        for dh, dp in everyone:
            sib_out[c, slot(dh, dp)] = partial(c, 2 * chip_at(dh, dp) + 1 - core).astype(BF16)
        sib_copy(c).start()

    def pass_on(c):
        for n, (dh, dp) in enumerate(reversed(everyone)):
            i = slot(dh, dp)
            value = partial(c, 2 * chip_at(dh, dp) + core)
            if n == 0:
                sib_copy(c).wait_recv()
            value = value + sib_in[c, i].astype(F32)
            if (dh, dp) == (0, 0):
                image[half, :, c * width : (c + 1) * width] = value
            else:
                far_out[c, i] = value.astype(BF16)
                far_copy(c, dh, dp).start()

    def collect(c):
        span = slice(c * width, (c + 1) * width)
        same = image[half, :, span]
        other = None
        for dh, dp in others:
            far_copy(c, dh, dp).wait_recv()
            value = far_in[c, slot(dh, dp)].astype(F32)
            if dh:
                other = value if other is None else other + value
            else:
                same = same + value
        image[half, :, span] = same
        image[1 - half, :, span] = other

    multiply(0)
    give(0)
    for c in range(1, cuts):
        multiply(c)
        give(c)
        pass_on(c - 1)
    pass_on(cuts - 1)
    for c in range(cuts):
        collect(c)

    spread = [jnp.zeros((rows, sector), F32) for _ in range(2 * HALO + 1)]
    for p in range(frames // 2):
        taps = coefs[p * pair : (p + 1) * pair, :].astype(F32)
        for i in range(2):
            f = 2 * p + i
            column = columns[f]
            g = f % (frames // 2)
            slices = image[f // (frames // 2), g * rows : (g + 1) * rows, :]
            for k in range(TAPS):
                start = (i * TAPS + k) * rows
                term = taps[start : start + rows] * slices
                for j in range(HALO + 1):
                    spread[k + j] = spread[k + j] + jnp.where(
                        column == float(j - HALO), term, 0.0
                    )
    total = None
    for m in range(2 * HALO + 1):
        pieces = [jnp.zeros((m, sector), F32)] if m else []
        pieces.append(spread[m])
        if m < 2 * HALO:
            pieces.append(jnp.zeros((2 * HALO - m, sector), F32))
        padded = jnp.concatenate(pieces, axis=0)
        total = padded if total is None else total + padded
    adj_out[0] = total[:HALO]
    adj_out[1] = total[rows + HALO :]
    exchange(adj_out, adj_in, ha_send, ha_recv)
    for j in range(2):
        for dh, dp in others:
            cross(dh, dp, j).wait_send()
        for dh, dp in everyone:
            to_sibling(dh, dp, j).wait_send()
    for copy in partner_copies:
        copy.wait_send()
    for n in range(parts):
        proj_copy(n).wait_send()
    wall_copy.wait_send()
    back_copy.wait()
    out_weighted.wait()
    for c in range(cuts):
        sib_copy(c).wait_send()
        for dh, dp in others:
            far_copy(c, dh, dp).wait_send()
    exchange_wait(adj_out, adj_in, ha_send, ha_recv)
    middle = jnp.zeros((rows - 2 * HALO, sector), F32)
    edges = jnp.concatenate([adj_in[0], middle, adj_in[1]], axis=0)
    adjoint = total[HALO : rows + HALO] + edges
    next_ref[...] = vol + voxel_weight[...] * adjoint
    out_next = pltpu.make_async_copy(next_ref, next_hbm, out_sem.at[1])
    out_next.start()
    out_next.wait()


def settle(next_in, weighted_in, next_out, weighted_out):
    next_out[...] = next_in[...]
    weighted_out[...] = weighted_in[...]


def body(
    volume,
    measured,
    tiles,
    tile_index,
    warp_coef,
    warp_offset,
    ray_weight,
    redundancy,
    conj_view,
    voxel_weight,
):
    frames, rows, rays = measured.shape
    sector = volume.shape[1]
    blocks = lax.axis_size("angle")
    slabs = lax.axis_size("frame")
    stacked = frames * rows
    chips = blocks // 2
    mine = tiles.shape[0] // 2
    parts = rays // 256
    cuts = 2
    vmem = pl.BlockSpec(memory_space=pltpu.VMEM)
    hbm = pl.BlockSpec(memory_space=pl.ANY)
    dma = pltpu.SemaphoreType.DMA
    flops = 4 * stacked * blocks * sector * rays
    volume_next, weighted = pl.pallas_call(
        functools.partial(kernel, blocks, slabs, frames, rows),
        out_shape=(
            jax.ShapeDtypeStruct(volume.shape, F32),
            jax.ShapeDtypeStruct((stacked, rays), BF16),
        ),
        in_specs=[hbm] * 10,
        out_specs=(hbm, hbm),
        scratch_shapes=[
            pltpu.VMEM(volume.shape, F32),
            pltpu.VMEM((stacked // 2, rays), BF16),
            pltpu.VMEM((frames * TAPS * rows, sector), BF16),
            pltpu.VMEM(warp_offset.shape, jnp.int32),
            pltpu.VMEM(ray_weight.shape, F32),
            pltpu.VMEM((rays,), F32),
            pltpu.VMEM(voxel_weight.shape, F32),
            pltpu.SMEM(tile_index.shape, jnp.int32),
            pltpu.SMEM(conj_view.shape, jnp.int32),
            pltpu.SMEM((4, mine), jnp.int32),
            pltpu.VMEM(volume.shape, F32),
            pltpu.VMEM((mine,) + tiles.shape[1:], BF16),
            pltpu.VMEM((blocks, 2, stacked // 4, sector), BF16),
            pltpu.VMEM((2, stacked // 4, sector), BF16),
            pltpu.VMEM((parts, stacked, 256), F32),
            pltpu.VMEM((parts, stacked, 256), F32),
            pltpu.VMEM((parts, stacked, 256), F32),
            pltpu.VMEM((stacked // 2, rays), BF16),
            pltpu.VMEM(ray_weight.shape, F32),
            pltpu.VMEM((rays,), F32),
            pltpu.VMEM((stacked, rays), BF16),
            pltpu.VMEM((stacked, rays), BF16),
            pltpu.VMEM((cuts, mine, 2 * stacked, sector // cuts), F32),
            pltpu.VMEM((2, stacked // 2, sector), F32),
            pltpu.VMEM((2, HALO, sector), F32),
            pltpu.VMEM((2, HALO, sector), F32),
            pltpu.VMEM((2, HALO, sector), F32),
            pltpu.VMEM((2, HALO, sector), F32),
            pltpu.VMEM((cuts, chips, stacked // 2, sector // cuts), BF16),
            pltpu.VMEM((cuts, chips, stacked // 2, sector // cuts), BF16),
            pltpu.VMEM((cuts, chips, stacked // 2, sector // cuts), BF16),
            pltpu.VMEM((cuts, chips, stacked // 2, sector // cuts), BF16),
            dma((9,)),
            dma((2,)),
            dma((mine,)),
            dma((chips, 2)),
            dma((chips, 2)),
            dma((chips, 2)),
            dma((chips, 2)),
            dma((3,)),
            dma((3,)),
            dma((parts,)),
            dma((parts,)),
            dma((2,)),
            dma((2,)),
            dma((2,)),
            dma((2,)),
            dma((2,)),
            dma((2,)),
            dma((cuts,)),
            dma((cuts,)),
            dma((cuts, chips)),
            dma((cuts, chips)),
        ],
        cost_estimate=pl.CostEstimate(
            flops=flops, bytes_accessed=2 * tiles.size, transcendentals=0
        ),
        compiler_params=pltpu.CompilerParams(
            collective_id=0, has_side_effects=True, vmem_limit_bytes=62 * 1024 * 1024
        ),
    )(
        volume,
        measured.reshape(stacked, rays),
        tiles,
        tile_index,
        warp_coef.reshape(frames * TAPS * rows, sector),
        warp_offset,
        ray_weight,
        redundancy,
        conj_view,
        voxel_weight,
    )
    volume_next, weighted = pl.pallas_call(
        settle,
        out_shape=(
            jax.ShapeDtypeStruct(volume.shape, F32),
            jax.ShapeDtypeStruct((stacked, rays), BF16),
        ),
        in_specs=[vmem, vmem],
        out_specs=(vmem, vmem),
    )(volume_next, weighted)
    return volume_next, weighted.reshape(frames, rows, rays)


def solution(mesh):
    placed = (
        P("frame", "angle"),
        P(None, "frame", "angle"),
        P(),
        P(),
        P(None, None, "frame", "angle"),
        P(None, "frame"),
        P("frame", "angle"),
        P("angle"),
        P("angle", None),
        P("frame", "angle"),
    )
    return jax.shard_map(
        body,
        mesh=mesh,
        in_specs=placed,
        out_specs=(P("frame", "angle"), P(None, "frame", "angle")),
        check_vma=False,
    )
```

```python
import functools

import jax
import jax.numpy as jnp
from jax import lax
from jax.experimental import pallas as pl
from jax.experimental.pallas import tpu as pltpu
from jax.sharding import PartitionSpec as P

VB = 2
HALO = 2
TAPS = 3
MESH = pl.DeviceIdType.MESH
F32 = jnp.float32
BF16 = jnp.bfloat16


def kernel(
    blocks,
    slabs,
    frames,
    rows,
    volume_hbm,
    measured_hbm,
    tiles_hbm,
    index_hbm,
    coefs_hbm,
    offsets_hbm,
    weight_hbm,
    red_hbm,
    conj_hbm,
    voxel_hbm,
    base_hbm,
    edges_hbm,
    weighted_hbm,
    volume,
    measured,
    coefs,
    offsets,
    ray_weight,
    redundancy,
    voxel_weight,
    tile_index,
    conj_view,
    find,
    base,
    zeros,
    tiles,
    turned,
    gathered,
    away,
    proj_mine,
    proj_out,
    proj_in,
    part_measured,
    part_weight,
    part_red,
    wall,
    wall_in,
    product,
    image,
    vol_out,
    vol_in,
    adj_out,
    sib_out,
    sib_in,
    far_out,
    far_in,
    in_sem,
    out_sem,
    zero_sem,
    tile_sem,
    ag_send,
    ag_recv,
    fw_send,
    fw_recv,
    pt_send,
    pt_recv,
    pj_send,
    pj_recv,
    wt_send,
    wt_recv,
    hv_send,
    hv_recv,
    ha_send,
    ha_recv,
    sb_send,
    sb_recv,
    fr_send,
    fr_recv,
):
    me = lax.axis_index("angle")
    slab = lax.axis_index("frame")
    chips = blocks // 2
    ring = chips // 2
    core = lax.rem(me, 2)
    chip = me // 2
    half = chip // ring
    place = lax.rem(chip, ring)
    sibling = me + 1 - 2 * core

    def chip_at(dh, dp):
        return lax.rem(half + dh, 2) * ring + lax.rem(place + dp, ring)

    def chip_from(dh, dp):
        return lax.rem(half + dh, 2) * ring + lax.rem(place + ring - dp, ring)

    partner = 2 * chip_at(1, 0) + core
    group = [me, partner, sibling, 2 * chip_at(1, 0) + 1 - core]
    others = [(dh, dp) for dp in range(ring) for dh in range(2) if dh or dp]
    everyone = [(0, 0)] + others
    count = tiles.shape[0]
    first = core * count
    stacked = frames * rows // 2
    sector = volume.shape[1]
    rays = measured.shape[1]
    view = rays // VB
    has_low = slab > 0
    has_high = slab < slabs - 1

    def remote(src, dst, send, recv, angle, frame=slab):
        return pltpu.make_async_remote_copy(
            src_ref=src,
            dst_ref=dst,
            send_sem=send,
            recv_sem=recv,
            device_id=(angle, frame),
            device_id_type=MESH,
        )

    def tile_copy(t):
        return pltpu.make_async_copy(tiles_hbm.at[first + t], tiles.at[t], tile_sem.at[t])

    barrier = pltpu.get_barrier_semaphore()
    pl.semaphore_signal(barrier, inc=1, device_id=(sibling, slab), device_id_type=MESH)
    for dh, dp in others:
        pl.semaphore_signal(
            barrier, inc=1, device_id=(2 * chip_at(dh, dp) + core, slab), device_id_type=MESH
        )

    @pl.when(has_low)
    def _():
        pl.semaphore_signal(barrier, inc=1, device_id=(me, slab - 1), device_id_type=MESH)

    @pl.when(has_high)
    def _():
        pl.semaphore_signal(barrier, inc=1, device_id=(me, slab + 1), device_id_type=MESH)

    measured_half = measured_hbm.at[pl.ds(pl.multiple_of(half * stacked, 16), stacked)]
    measured_away = measured_hbm.at[pl.ds(pl.multiple_of((1 - half) * stacked, 16), stacked)]
    local = [
        pltpu.make_async_copy(src, dst, in_sem.at[n])
        for n, (src, dst) in enumerate(
            (
                (volume_hbm, volume),
                (coefs_hbm, coefs),
                (offsets_hbm, offsets),
                (index_hbm, tile_index),
                (conj_hbm, conj_view),
                (measured_half, measured),
                (weight_hbm, ray_weight),
                (red_hbm, redundancy),
                (voxel_hbm, voxel_weight),
            )
        )
    ]
    for copy in local:
        copy.start()
    for t in range(count):
        tile_copy(t).start()
    local[0].wait()
    vol = volume[...]
    vol_out[0] = vol[:HALO]
    vol_out[1] = vol[rows - HALO :]

    peers = chips + has_low.astype(jnp.int32) + has_high.astype(jnp.int32)
    pl.semaphore_wait(barrier, peers)

    def halo(out, into, send, recv, side):
        return remote(
            out.at[side], into.at[1 - side], send.at[side], recv.at[1 - side], me, slab + 2 * side - 1
        )

    def exchange(out, into, send, recv):
        @pl.when(has_low)
        def _():
            halo(out, into, send, recv, 0).start()

        @pl.when(has_high)
        def _():
            halo(out, into, send, recv, 1).start()

    def exchange_wait(out, into, send, recv):
        @pl.when(has_low)
        def _():
            halo(out, into, send, recv, 0).wait_send()
            halo(out, into, send, recv, 1).wait_recv()

        @pl.when(has_high)
        def _():
            halo(out, into, send, recv, 1).wait_send()
            halo(out, into, send, recv, 0).wait_recv()

    exchange(vol_out, vol_in, hv_send, hv_recv)
    local[1].wait()
    local[2].wait()

    off = offsets[...].astype(F32)
    lane = lax.broadcasted_iota(jnp.int32, (rows, rows), 1)
    diagonal = lane == lax.broadcasted_iota(jnp.int32, (rows, rows), 0)

    def offset_column(f):
        spread = jnp.broadcast_to(off[f : f + 1, :], (rows, rows))
        return jnp.sum(jnp.where(diagonal, spread, 0.0), axis=1, keepdims=True)

    columns = [offset_column(f) for f in range(frames)]
    pair = 2 * TAPS * rows

    def warp(below, above):
        extended = jnp.concatenate([below, vol, above], axis=0)
        sources = [extended[m : m + rows] for m in range(2 * HALO + 1)]
        warped = []
        for p in range(frames // 2):
            taps = coefs[p * pair : (p + 1) * pair, :].astype(F32)
            for i in range(2):
                column = columns[2 * p + i]
                low = column == -2.0
                mid = column == -1.0
                total = None
                for k in range(TAPS):
                    start = (i * TAPS + k) * rows
                    chosen = jnp.where(
                        low, sources[k], jnp.where(mid, sources[k + 1], sources[k + 2])
                    )
                    term = taps[start : start + rows] * chosen
                    total = term if total is None else total + term
                warped.append(total)
        return warped

    def keep(j, pieces):
        each = len(pieces) // 2
        early = jnp.concatenate(pieces[:each], axis=0)
        late = jnp.concatenate(pieces[each:], axis=0)
        gathered[me, j] = jnp.where(half == 0, early, late).astype(BF16)
        away[j] = jnp.where(half == 0, late, early).astype(BF16)

    def slot(dh, dp):
        return dh * ring + dp

    def cross(dh, dp, j):
        return remote(
            away.at[j] if dh else gathered.at[me, j],
            gathered.at[me, j],
            ag_send.at[slot(dh, dp), j],
            ag_recv.at[slot(dh, dp), j],
            2 * chip_at(dh, dp) + core,
        )

    def to_sibling(dh, dp, j):
        block = 2 * chip_from(dh, dp) + core
        return remote(
            gathered.at[block, j],
            gathered.at[block, j],
            fw_send.at[slot(dh, dp), j],
            fw_recv.at[slot(dh, dp), j],
            sibling,
        )

    def spread_chunk(j):
        for dh, dp in reversed(others):
            cross(dh, dp, j).start()
        to_sibling(0, 0, j).start()

    def pass_chunk(j):
        for dh, dp in others:
            cross(dh, dp, j).wait_recv()
            to_sibling(dh, dp, j).start()

    partner_copies = [
        remote(measured_away, part_measured, pt_send.at[0], pt_recv.at[0], partner),
        remote(weight_hbm, part_weight, pt_send.at[1], pt_recv.at[1], partner),
        remote(red_hbm, part_red, pt_send.at[2], pt_recv.at[2], partner),
    ]
    block = 128

    def turn(t):
        tile_copy(t).wait()

        def step(n, carry):
            span = pl.ds(pl.multiple_of(n * block, block), block)
            turned[t, :, span] = tiles[t, span, :].T
            return carry

        lax.fori_loop(0, sector // block, step, 0)

    outside = jnp.zeros((HALO, sector), F32)
    keep(0, [value[HALO : rows - HALO] for value in warp(outside, outside)])
    spread_chunk(0)
    turn(0)
    for copy in partner_copies[1:]:
        copy.start()
    exchange_wait(vol_out, vol_in, hv_send, hv_recv)

    @pl.when(slab == 0)
    def _():
        vol_in[0] = jnp.zeros_like(vol_in[0])
        zeros[...] = jnp.zeros_like(zeros)
        pltpu.make_async_copy(zeros, edges_hbm.at[0], zero_sem.at[0]).start()

    @pl.when(slab == slabs - 1)
    def _():
        vol_in[1] = jnp.zeros_like(vol_in[1])
        zeros[...] = jnp.zeros_like(zeros)
        pltpu.make_async_copy(zeros, edges_hbm.at[1], zero_sem.at[0]).start()

    outer = []
    for value in warp(vol_in[0], vol_in[1]):
        outer += [jnp.concatenate([value[:HALO], value[rows - HALO :]], axis=0)]
    keep(1, outer)
    spread_chunk(1)
    partner_copies[0].start()
    turn(1)

    local[3].wait()
    for q in range(4):
        row = [tile_index[group[q], s] for s in range(blocks)]
        for t in range(count):
            at = jnp.int32(0)
            for s in range(blocks):
                at = jnp.where(row[s] == first + t, s, at)
            find[q, t] = at

    pass_chunk(0)
    turn(2)
    pass_chunk(1)
    for t in range(turned.shape[0], count):
        tile_copy(t).wait()
    for j in range(2):
        for dh, dp in everyone:
            to_sibling(dh, dp, j).wait_recv()

    def proj_copy(w):
        return remote(proj_out.at[w], proj_in.at[w], pj_send.at[w], pj_recv.at[w], sibling)

    for w in range(VB):
        total = None
        for t in range(count):
            left = jnp.concatenate(
                [gathered[find[q, t]].reshape(stacked, sector) for q in range(4)], axis=0
            )
            term = jnp.dot(
                left, tiles[t, :, w * view : (w + 1) * view], preferred_element_type=F32
            )
            total = term if total is None else total + term
        proj_mine[w] = total[: 2 * stacked]
        proj_out[w] = total[2 * stacked :]

    for w in range(VB):
        proj_copy(w).start()
    for copy in local[4:]:
        copy.wait()
    for copy in partner_copies:
        copy.wait_recv()

    inside = rows - 2 * HALO
    chunk = frames * inside // 2

    def in_order(value, base):
        pieces = []
        for f in range(frames // 2):
            a = base + f * inside
            b = base + chunk + f * 2 * HALO
            pieces += [value[b : b + HALO], value[a : a + inside], value[b + HALO : b + 2 * HALO]]
        return jnp.concatenate(pieces, axis=0)

    wide = 256
    each = view // wide
    flip = lax.broadcasted_iota(jnp.int32, (wide, wide), 0) + lax.broadcasted_iota(
        jnp.int32, (wide, wide), 1
    )
    flip = jnp.where(flip == wide - 1, 1.0, 0.0).astype(BF16)
    swap = conj_view[0, 0] == 1
    residuals = []
    flipped = []
    for w in range(VB):
        span = slice(w * view, (w + 1) * view)
        proj_copy(w).wait_recv()
        value = proj_mine[w] + proj_in[w]
        value = jnp.concatenate(
            [
                measured[:, span].astype(F32) - in_order(value, 0),
                part_measured[:, span].astype(F32) - in_order(value, stacked),
            ],
            axis=0,
        )
        residuals.append(value)
        tall = jnp.concatenate(
            [value[:, u * wide : (u + 1) * wide] for u in reversed(range(each))], axis=0
        )
        high = tall.astype(BF16)
        rest = (tall - high.astype(F32)).astype(BF16)
        tall = jnp.dot(high, flip, preferred_element_type=F32) + jnp.dot(
            rest, flip, preferred_element_type=F32
        )
        flipped.append(
            jnp.concatenate(
                [tall[u * 2 * stacked : (u + 1) * 2 * stacked] for u in range(each)], axis=1
            )
        )

    def combine(residual, mirrored, red, weight):
        red = jnp.broadcast_to(red, residual.shape)
        value = red * residual + (1.0 - red) * mirrored
        return (value * jnp.concatenate([weight] * (frames // 2), axis=0)).astype(BF16)

    def wall_copy(w):
        return remote(wall.at[w], wall_in.at[w], wt_send.at[0, w], wt_recv.at[0, w], sibling)

    place_rows = pl.ds(pl.multiple_of(half * stacked, 16), stacked)

    def out_weighted(w):
        return pltpu.make_async_copy(
            wall.at[w, pl.ds(0, stacked)],
            weighted_hbm.at[place_rows, pl.ds(w * view, view)],
            out_sem.at[1 + w],
        )

    def back_copy(w):
        return remote(
            wall.at[w, pl.ds(stacked, stacked)],
            weighted_hbm.at[place_rows, pl.ds(w * view, view)],
            wt_send.at[1, w],
            wt_recv.at[1, w],
            partner,
        )

    red_own = redundancy[...][None, :]
    red_part = part_red[...][None, :]
    for w in range(VB):
        span = slice(w * view, (w + 1) * view)
        mirrored = jnp.where(swap, flipped[VB - 1 - w], flipped[w])
        wall[w, :stacked] = combine(
            residuals[w][:stacked], mirrored[stacked:], red_own[:, span], ray_weight[:, span]
        )
        wall[w, stacked:] = combine(
            residuals[w][stacked:], mirrored[:stacked], red_part[:, span], part_weight[:, span]
        )
        wall_copy(w).start()
    for w in range(VB):
        back_copy(w).start()
        out_weighted(w).start()

    cuts = product.shape[0]
    width = sector // cuts

    def multiply():
        for t in range(count):
            total = None
            for w in range(VB):
                both = jnp.concatenate([wall[w], wall_in[w]], axis=0)
                cut = slice(w * view, (w + 1) * view)
                if t < turned.shape[0]:
                    value = jnp.dot(both, turned[t, cut, :], preferred_element_type=F32)
                else:
                    value = lax.dot_general(
                        both,
                        tiles[t, :, cut],
                        (((1,), (1,)), ((), ())),
                        preferred_element_type=F32,
                    )
                total = value if total is None else total + value
            for c in range(cuts):
                product[c, t] = total[:, c * width : (c + 1) * width]

    def partial(c, s):
        total = None
        for q in range(4):
            t = tile_index[group[q], s] - first
            ours = jnp.logical_and(t >= 0, t < count)
            t = jnp.where(ours, t, 0)
            term = jnp.where(ours, product[c, t, q * stacked : (q + 1) * stacked, :], 0.0)
            total = term if total is None else total + term
        return total

    def sib_copy(c):
        return remote(sib_out.at[c], sib_in.at[c], sb_send.at[c], sb_recv.at[c], sibling)

    def far_copy(c, dh, dp):
        i = slot(dh, dp)
        return remote(
            far_out.at[c, i],
            far_in.at[c, i],
            fr_send.at[c, i],
            fr_recv.at[c, i],
            2 * chip_at(dh, dp) + core,
        )

    def give(c):
        for dh, dp in everyone:
            sib_out[c, slot(dh, dp)] = partial(c, 2 * chip_at(dh, dp) + 1 - core).astype(BF16)
        sib_copy(c).start()

    def pass_on(c):
        for n, (dh, dp) in enumerate(reversed(everyone)):
            i = slot(dh, dp)
            value = partial(c, 2 * chip_at(dh, dp) + core)
            if n == 0:
                sib_copy(c).wait_recv()
            value = value + sib_in[c, i].astype(F32)
            if (dh, dp) == (0, 0):
                image[half, :, c * width : (c + 1) * width] = value
            else:
                far_out[c, i] = value.astype(BF16)
                far_copy(c, dh, dp).start()

    def collect(c):
        span = slice(c * width, (c + 1) * width)
        same = image[half, :, span]
        other = None
        for dh, dp in others:
            far_copy(c, dh, dp).wait_recv()
            value = far_in[c, slot(dh, dp)].astype(F32)
            if dh:
                other = value if other is None else other + value
            else:
                same = same + value
        image[half, :, span] = same
        image[1 - half, :, span] = other

    for w in range(VB):
        wall_copy(w).wait_recv()
    multiply()
    for c in range(cuts):
        give(c)
    for c in range(cuts - 1):
        pass_on(c)
    pass_on(cuts - 1)

    totals = []
    for c in range(cuts):
        collect(c)
        span = slice(c * width, (c + 1) * width)
        spread = [jnp.zeros((rows, width), F32) for _ in range(2 * HALO + 1)]
        for p in range(frames // 2):
            taps = coefs[p * pair : (p + 1) * pair, span].astype(F32)
            for i in range(2):
                f = 2 * p + i
                column = columns[f]
                g = f % (frames // 2)
                slices = image[f // (frames // 2), g * rows : (g + 1) * rows, span]
                for k in range(TAPS):
                    start = (i * TAPS + k) * rows
                    term = taps[start : start + rows] * slices
                    for j in range(HALO + 1):
                        spread[k + j] = spread[k + j] + jnp.where(
                            column == float(j - HALO), term, 0.0
                        )
        total = None
        for m in range(2 * HALO + 1):
            pieces = [jnp.zeros((m, width), F32)] if m else []
            pieces.append(spread[m])
            if m < 2 * HALO:
                pieces.append(jnp.zeros((2 * HALO - m, width), F32))
            padded = jnp.concatenate(pieces, axis=0)
            total = padded if total is None else total + padded
        adj_out[0, :, span] = total[:HALO]
        adj_out[1, :, span] = total[rows + HALO :]
        totals.append(total[HALO : rows + HALO])
    exchange(adj_out, edges_hbm, ha_send, ha_recv)
    base[...] = vol + voxel_weight[...] * jnp.concatenate(totals, axis=1)
    out_base = pltpu.make_async_copy(base, base_hbm, out_sem.at[0])
    out_base.start()
    for j in range(2):
        for dh, dp in others:
            cross(dh, dp, j).wait_send()
        for dh, dp in everyone:
            to_sibling(dh, dp, j).wait_send()
    for copy in partner_copies:
        copy.wait_send()
    for w in range(VB):
        proj_copy(w).wait_send()
        wall_copy(w).wait_send()
        back_copy(w).wait()
        out_weighted(w).wait()
    for c in range(cuts):
        sib_copy(c).wait_send()
        for dh, dp in others:
            far_copy(c, dh, dp).wait_send()

    @pl.when(slab == 0)
    def _():
        pltpu.make_async_copy(zeros, edges_hbm.at[0], zero_sem.at[0]).wait()

    @pl.when(slab == slabs - 1)
    def _():
        pltpu.make_async_copy(zeros, edges_hbm.at[1], zero_sem.at[0]).wait()

    out_base.wait()
    exchange_wait(adj_out, edges_hbm, ha_send, ha_recv)


def settle(
    base_in,
    edges_in,
    scale_in,
    weighted_in,
    next_out,
    weighted_out,
    base,
    edges,
    scale,
    rows,
    in_sem,
    out_sem,
):
    loads = [
        pltpu.make_async_copy(src, dst, in_sem.at[n])
        for n, (src, dst) in enumerate(
            ((weighted_in, rows), (base_in, base), (edges_in, edges), (scale_in, scale))
        )
    ]
    for load in loads:
        load.start()
    out_rows = pltpu.make_async_copy(rows, weighted_out, out_sem.at[0])
    out_next = pltpu.make_async_copy(base, next_out, out_sem.at[1])
    loads[0].wait()
    out_rows.start()
    for load in loads[1:]:
        load.wait()
    middle = jnp.zeros((base.shape[0] - 2 * HALO, base.shape[1]), F32)
    adjoint = jnp.concatenate([edges[0], middle, edges[1]], axis=0)
    base[...] = base[...] + scale[...] * adjoint
    out_next.start()
    out_rows.wait()
    out_next.wait()


def body(
    volume,
    measured,
    tiles,
    tile_index,
    warp_coef,
    warp_offset,
    ray_weight,
    redundancy,
    conj_view,
    voxel_weight,
):
    frames, rows, rays = measured.shape
    sector = volume.shape[1]
    blocks = lax.axis_size("angle")
    slabs = lax.axis_size("frame")
    stacked = frames * rows
    chips = blocks // 2
    mine = tiles.shape[0] // 2
    view = rays // VB
    cuts = 2
    hbm = pl.BlockSpec(memory_space=pl.ANY)
    dma = pltpu.SemaphoreType.DMA
    flops = 4 * stacked * blocks * sector * rays
    base, edges, weighted = pl.pallas_call(
        functools.partial(kernel, blocks, slabs, frames, rows),
        out_shape=(
            jax.ShapeDtypeStruct(volume.shape, F32),
            jax.ShapeDtypeStruct((2, HALO, sector), F32),
            jax.ShapeDtypeStruct((stacked, rays), BF16),
        ),
        in_specs=[hbm] * 10,
        out_specs=(hbm, hbm, hbm),
        scratch_shapes=[
            pltpu.VMEM(volume.shape, F32),
            pltpu.VMEM((stacked // 2, rays), BF16),
            pltpu.VMEM((frames * TAPS * rows, sector), BF16),
            pltpu.VMEM(warp_offset.shape, jnp.int32),
            pltpu.VMEM(ray_weight.shape, F32),
            pltpu.VMEM((rays,), F32),
            pltpu.VMEM(voxel_weight.shape, F32),
            pltpu.SMEM(tile_index.shape, jnp.int32),
            pltpu.SMEM(conj_view.shape, jnp.int32),
            pltpu.SMEM((4, mine), jnp.int32),
            pltpu.VMEM(volume.shape, F32),
            pltpu.VMEM((HALO, sector), F32),
            pltpu.VMEM((mine,) + tiles.shape[1:], BF16),
            pltpu.VMEM((3, rays, sector), BF16),
            pltpu.VMEM((blocks, 2, stacked // 4, sector), BF16),
            pltpu.VMEM((2, stacked // 4, sector), BF16),
            pltpu.VMEM((VB, stacked, view), F32),
            pltpu.VMEM((VB, stacked, view), F32),
            pltpu.VMEM((VB, stacked, view), F32),
            pltpu.VMEM((stacked // 2, rays), BF16),
            pltpu.VMEM(ray_weight.shape, F32),
            pltpu.VMEM((rays,), F32),
            pltpu.VMEM((VB, stacked, view), BF16),
            pltpu.VMEM((VB, stacked, view), BF16),
            pltpu.VMEM((cuts, mine, 2 * stacked, sector // cuts), F32),
            pltpu.VMEM((2, stacked // 2, sector), F32),
            pltpu.VMEM((2, HALO, sector), F32),
            pltpu.VMEM((2, HALO, sector), F32),
            pltpu.VMEM((2, HALO, sector), F32),
            pltpu.VMEM((cuts, chips, stacked // 2, sector // cuts), BF16),
            pltpu.VMEM((cuts, chips, stacked // 2, sector // cuts), BF16),
            pltpu.VMEM((cuts, chips, stacked // 2, sector // cuts), BF16),
            pltpu.VMEM((cuts, chips, stacked // 2, sector // cuts), BF16),
            dma((9,)),
            dma((1 + VB,)),
            dma((1,)),
            dma((mine,)),
            dma((chips, 2)),
            dma((chips, 2)),
            dma((chips, 2)),
            dma((chips, 2)),
            dma((3,)),
            dma((3,)),
            dma((VB,)),
            dma((VB,)),
            dma((2, VB)),
            dma((2, VB)),
            dma((2,)),
            dma((2,)),
            dma((2,)),
            dma((2,)),
            dma((cuts,)),
            dma((cuts,)),
            dma((cuts, chips)),
            dma((cuts, chips)),
        ],
        cost_estimate=pl.CostEstimate(
            flops=flops, bytes_accessed=2 * tiles.size, transcendentals=0
        ),
        compiler_params=pltpu.CompilerParams(
            collective_id=0, has_side_effects=True, vmem_limit_bytes=62 * 1024 * 1024
        ),
    )(
        volume,
        measured.reshape(stacked, rays),
        tiles,
        tile_index,
        warp_coef.reshape(frames * TAPS * rows, sector),
        warp_offset,
        ray_weight,
        redundancy,
        conj_view,
        voxel_weight,
    )
    volume_next, weighted = pl.pallas_call(
        settle,
        out_shape=(
            jax.ShapeDtypeStruct(volume.shape, F32),
            jax.ShapeDtypeStruct((stacked, rays), BF16),
        ),
        in_specs=[hbm] * 4,
        out_specs=(hbm, hbm),
        scratch_shapes=[
            pltpu.VMEM(volume.shape, F32),
            pltpu.VMEM((2, HALO, sector), F32),
            pltpu.VMEM(volume.shape, F32),
            pltpu.VMEM((stacked, rays), BF16),
            dma((4,)),
            dma((2,)),
        ],
    )(base, edges, voxel_weight, weighted)
    return volume_next, weighted.reshape(frames, rows, rays)


def solution(mesh):
    placed = (
        P("frame", "angle"),
        P(None, "frame", "angle"),
        P(),
        P(),
        P(None, None, "frame", "angle"),
        P(None, "frame"),
        P("frame", "angle"),
        P("angle"),
        P("angle", None),
        P("frame", "angle"),
    )
    return jax.shard_map(
        body,
        mesh=mesh,
        in_specs=placed,
        out_specs=(P("frame", "angle"), P(None, "frame", "angle")),
        check_vma=False,
    )
```

```python
import functools

import jax
import jax.numpy as jnp
from jax import lax
from jax.experimental import pallas as pl
from jax.experimental.pallas import tpu as pltpu
from jax.sharding import PartitionSpec as P

VB = 2
HALO = 2
TAPS = 3
MESH = pl.DeviceIdType.MESH
F32 = jnp.float32
BF16 = jnp.bfloat16


def kernel(
    blocks,
    slabs,
    frames,
    rows,
    volume_hbm,
    measured_hbm,
    tiles_hbm,
    index_hbm,
    coefs_hbm,
    offsets_hbm,
    weight_hbm,
    red_hbm,
    conj_hbm,
    voxel_hbm,
    base_hbm,
    edges_hbm,
    weighted_hbm,
    volume,
    measured,
    coefs,
    offsets,
    ray_weight,
    redundancy,
    voxel_weight,
    tile_index,
    conj_view,
    find,
    pick,
    base,
    zeros,
    omega,
    tiles,
    turned,
    gathered,
    away,
    proj_mine,
    proj_out,
    proj_in,
    part_measured,
    part_weight,
    part_red,
    wall,
    wall_in,
    product,
    image,
    vol_out,
    vol_in,
    adj_out,
    sib_out,
    sib_in,
    far_out,
    far_in,
    in_sem,
    out_sem,
    zero_sem,
    tile_sem,
    ag_send,
    ag_recv,
    fw_send,
    fw_recv,
    pt_send,
    pt_recv,
    pj_send,
    pj_recv,
    wt_send,
    wt_recv,
    hv_send,
    hv_recv,
    ha_send,
    ha_recv,
    sb_send,
    sb_recv,
    fr_send,
    fr_recv,
):
    me = lax.axis_index("angle")
    slab = lax.axis_index("frame")
    chips = blocks // 2
    ring = chips // 2
    core = lax.rem(me, 2)
    chip = me // 2
    half = chip // ring
    place = lax.rem(chip, ring)
    sibling = me + 1 - 2 * core

    def chip_at(dh, dp):
        return lax.rem(half + dh, 2) * ring + lax.rem(place + dp, ring)

    def chip_from(dh, dp):
        return lax.rem(half + dh, 2) * ring + lax.rem(place + ring - dp, ring)

    partner = 2 * chip_at(1, 0) + core
    group = [me, partner, sibling, 2 * chip_at(1, 0) + 1 - core]
    others = [(dh, dp) for dp in range(ring) for dh in range(2) if dh or dp]
    everyone = [(0, 0)] + others
    count = tiles.shape[0]
    first = core * count
    stacked = frames * rows // 2
    sector = volume.shape[1]
    rays = measured.shape[1]
    view = rays // VB
    has_low = slab > 0
    has_high = slab < slabs - 1

    def remote(src, dst, send, recv, angle, frame=slab):
        return pltpu.make_async_remote_copy(
            src_ref=src,
            dst_ref=dst,
            send_sem=send,
            recv_sem=recv,
            device_id=(angle, frame),
            device_id_type=MESH,
        )

    def tile_copy(t):
        return pltpu.make_async_copy(tiles_hbm.at[first + t], tiles.at[t], tile_sem.at[t])

    barrier = pltpu.get_barrier_semaphore()
    pl.semaphore_signal(barrier, inc=1, device_id=(sibling, slab), device_id_type=MESH)
    for dh, dp in others:
        for other in (core, 1 - core):
            pl.semaphore_signal(
                barrier, inc=1, device_id=(2 * chip_at(dh, dp) + other, slab), device_id_type=MESH
            )

    @pl.when(has_low)
    def _():
        pl.semaphore_signal(barrier, inc=1, device_id=(me, slab - 1), device_id_type=MESH)

    @pl.when(has_high)
    def _():
        pl.semaphore_signal(barrier, inc=1, device_id=(me, slab + 1), device_id_type=MESH)

    measured_half = measured_hbm.at[pl.ds(pl.multiple_of(half * stacked, 16), stacked)]
    measured_away = measured_hbm.at[pl.ds(pl.multiple_of((1 - half) * stacked, 16), stacked)]
    local = [
        pltpu.make_async_copy(src, dst, in_sem.at[n])
        for n, (src, dst) in enumerate(
            (
                (volume_hbm, volume),
                (coefs_hbm, coefs),
                (offsets_hbm, offsets),
                (index_hbm, tile_index),
                (conj_hbm, conj_view),
                (measured_half, measured),
                (weight_hbm, ray_weight),
                (red_hbm, redundancy),
                (voxel_hbm, voxel_weight),
            )
        )
    ]
    for copy in local:
        copy.start()
    for t in range(count):
        tile_copy(t).start()
    local[0].wait()
    vol = volume[...]
    vol_out[0] = vol[:HALO]
    vol_out[1] = vol[rows - HALO :]

    peers = blocks - 1 + has_low.astype(jnp.int32) + has_high.astype(jnp.int32)
    pl.semaphore_wait(barrier, peers)

    def halo(out, into, send, recv, side):
        return remote(
            out.at[side], into.at[1 - side], send.at[side], recv.at[1 - side], me, slab + 2 * side - 1
        )

    def exchange(out, into, send, recv):
        @pl.when(has_low)
        def _():
            halo(out, into, send, recv, 0).start()

        @pl.when(has_high)
        def _():
            halo(out, into, send, recv, 1).start()

    def exchange_wait(out, into, send, recv):
        @pl.when(has_low)
        def _():
            halo(out, into, send, recv, 0).wait_send()
            halo(out, into, send, recv, 1).wait_recv()

        @pl.when(has_high)
        def _():
            halo(out, into, send, recv, 1).wait_send()
            halo(out, into, send, recv, 0).wait_recv()

    exchange(vol_out, vol_in, hv_send, hv_recv)
    local[1].wait()
    local[2].wait()

    off = offsets[...].astype(F32)
    lane = lax.broadcasted_iota(jnp.int32, (rows, rows), 1)
    diagonal = lane == lax.broadcasted_iota(jnp.int32, (rows, rows), 0)

    def offset_column(f):
        spread = jnp.broadcast_to(off[f : f + 1, :], (rows, rows))
        return jnp.sum(jnp.where(diagonal, spread, 0.0), axis=1, keepdims=True)

    columns = [offset_column(f) for f in range(frames)]
    pair = 2 * TAPS * rows

    def warp(below, above):
        extended = jnp.concatenate([below, vol, above], axis=0)
        sources = [extended[m : m + rows] for m in range(2 * HALO + 1)]
        warped = []
        for p in range(frames // 2):
            taps = coefs[p * pair : (p + 1) * pair, :].astype(F32)
            for i in range(2):
                column = columns[2 * p + i]
                low = column == -2.0
                mid = column == -1.0
                total = None
                for k in range(TAPS):
                    start = (i * TAPS + k) * rows
                    chosen = jnp.where(
                        low, sources[k], jnp.where(mid, sources[k + 1], sources[k + 2])
                    )
                    term = taps[start : start + rows] * chosen
                    total = term if total is None else total + term
                warped.append(total)
        return warped

    def keep(j, pieces):
        each = len(pieces) // 2
        early = jnp.concatenate(pieces[:each], axis=0)
        late = jnp.concatenate(pieces[each:], axis=0)
        gathered[me, j] = jnp.where(half == 0, early, late).astype(BF16)
        away[j] = jnp.where(half == 0, late, early).astype(BF16)

    def slot(dh, dp):
        return dh * ring + dp

    def cross(dh, dp, j):
        return remote(
            away.at[j] if dh else gathered.at[me, j],
            gathered.at[me, j],
            ag_send.at[slot(dh, dp) - 1, j],
            ag_recv.at[slot(dh, dp) - 1, j],
            2 * chip_at(dh, dp) + core,
        )

    def to_sibling(dh, dp, j):
        block = 2 * chip_from(dh, dp) + core
        return remote(
            gathered.at[block, j],
            gathered.at[block, j],
            fw_send.at[slot(dh, dp), j],
            fw_recv.at[slot(dh, dp), j],
            sibling,
        )

    def spread_chunk(j):
        for dh, dp in reversed(others):
            cross(dh, dp, j).start()
        to_sibling(0, 0, j).start()

    def pass_chunk(j):
        for dh, dp in others:
            cross(dh, dp, j).wait_recv()
            to_sibling(dh, dp, j).start()

    partner_copies = [
        remote(measured_away, part_measured, pt_send.at[0], pt_recv.at[0], partner),
        remote(weight_hbm, part_weight, pt_send.at[1], pt_recv.at[1], partner),
        remote(red_hbm, part_red, pt_send.at[2], pt_recv.at[2], partner),
    ]
    block = 128

    def turn(t):
        tile_copy(t).wait()

        def step(n, carry):
            span = pl.ds(pl.multiple_of(n * block, block), block)
            turned[t, :, span] = tiles[t, span, :].T
            return carry

        lax.fori_loop(0, sector // block, step, 0)

    outside = jnp.zeros((HALO, sector), F32)
    keep(0, [value[HALO : rows - HALO] for value in warp(outside, outside)])
    spread_chunk(0)
    turn(0)
    for copy in partner_copies[1:]:
        copy.start()
    exchange_wait(vol_out, vol_in, hv_send, hv_recv)

    @pl.when(slab == 0)
    def _():
        vol_in[0] = jnp.zeros_like(vol_in[0])
        zeros[...] = jnp.zeros_like(zeros)
        pltpu.make_async_copy(zeros, edges_hbm.at[0], zero_sem.at[0]).start()

    @pl.when(slab == slabs - 1)
    def _():
        vol_in[1] = jnp.zeros_like(vol_in[1])
        zeros[...] = jnp.zeros_like(zeros)
        pltpu.make_async_copy(zeros, edges_hbm.at[1], zero_sem.at[0]).start()

    outer = []
    for value in warp(vol_in[0], vol_in[1]):
        outer += [jnp.concatenate([value[:HALO], value[rows - HALO :]], axis=0)]
    keep(1, outer)
    spread_chunk(1)
    partner_copies[0].start()
    turn(1)

    local[3].wait()
    for q in range(4):
        row = [tile_index[group[q], s] for s in range(blocks)]
        for t in range(count):
            at = jnp.int32(0)
            for s in range(blocks):
                at = jnp.where(row[s] == first + t, s, at)
            find[q, t] = at
    for i, (dh, dp) in enumerate(everyone):
        for n in range(2):
            s = 2 * chip_at(dh, dp) + (core if bool(n) == (i == 0) else 1 - core)
            for q in range(4):
                t = tile_index[group[q], s] - first
                ours = jnp.logical_and(t >= 0, t < count)
                pick[2 * i + n, q] = jnp.where(ours, t, count)

    pass_chunk(0)
    turn(2)
    pass_chunk(1)
    for t in range(turned.shape[0], count):
        tile_copy(t).wait()
    for j in range(2):
        for dh, dp in everyone:
            to_sibling(dh, dp, j).wait_recv()

    def proj_copy(w):
        return remote(proj_out.at[w], proj_in.at[w], pj_send.at[w], pj_recv.at[w], sibling)

    for w in range(VB):
        total = None
        for t in range(count):
            left = jnp.concatenate(
                [gathered[find[q, t]].reshape(stacked, sector) for q in range(4)], axis=0
            )
            term = jnp.dot(
                left, tiles[t, :, w * view : (w + 1) * view], preferred_element_type=F32
            )
            total = term if total is None else total + term
        proj_mine[w] = total[: 2 * stacked]
        proj_out[w] = total[2 * stacked :]

    for w in range(VB):
        proj_copy(w).start()
    product[:, count] = jnp.zeros_like(product[:, count])
    for copy in local[4:]:
        copy.wait()
    for copy in partner_copies:
        copy.wait_recv()

    inside = rows - 2 * HALO
    chunk = frames * inside // 2

    def in_order(value, base):
        pieces = []
        for f in range(frames // 2):
            a = base + f * inside
            b = base + chunk + f * 2 * HALO
            pieces += [value[b : b + HALO], value[a : a + inside], value[b + HALO : b + 2 * HALO]]
        return jnp.concatenate(pieces, axis=0)

    wide = 256
    each = view // wide
    flip = lax.broadcasted_iota(jnp.int32, (wide, wide), 0) + lax.broadcasted_iota(
        jnp.int32, (wide, wide), 1
    )
    flip = jnp.where(flip == wide - 1, 1.0, 0.0).astype(BF16)
    swap = conj_view[0, 0] == 1
    residuals = []
    flipped = []
    for w in range(VB):
        span = slice(w * view, (w + 1) * view)
        proj_copy(w).wait_recv()
        value = proj_mine[w] + proj_in[w]
        value = jnp.concatenate(
            [
                measured[:, span].astype(F32) - in_order(value, 0),
                part_measured[:, span].astype(F32) - in_order(value, stacked),
            ],
            axis=0,
        )
        residuals.append(value)
        tall = jnp.concatenate(
            [value[:, u * wide : (u + 1) * wide] for u in reversed(range(each))], axis=0
        )
        high = tall.astype(BF16)
        rest = (tall - high.astype(F32)).astype(BF16)
        tall = jnp.dot(high, flip, preferred_element_type=F32) + jnp.dot(
            rest, flip, preferred_element_type=F32
        )
        flipped.append(
            jnp.concatenate(
                [tall[u * 2 * stacked : (u + 1) * 2 * stacked] for u in range(each)], axis=1
            )
        )

    def combine(residual, mirrored, red, weight):
        red = jnp.broadcast_to(red, residual.shape)
        value = red * residual + (1.0 - red) * mirrored
        return (value * jnp.concatenate([weight] * (frames // 2), axis=0)).astype(BF16)

    def wall_copy(w):
        return remote(wall.at[w], wall_in.at[w], wt_send.at[0, w], wt_recv.at[0, w], sibling)

    place_rows = pl.ds(pl.multiple_of(half * stacked, 16), stacked)

    def out_weighted(w):
        return pltpu.make_async_copy(
            wall.at[w, pl.ds(0, stacked)],
            weighted_hbm.at[place_rows, pl.ds(w * view, view)],
            out_sem.at[1 + w],
        )

    def back_copy(w):
        return remote(
            wall.at[w, pl.ds(stacked, stacked)],
            weighted_hbm.at[place_rows, pl.ds(w * view, view)],
            wt_send.at[1, w],
            wt_recv.at[1, w],
            partner,
        )

    red_own = redundancy[...][None, :]
    red_part = part_red[...][None, :]
    for w in range(VB):
        span = slice(w * view, (w + 1) * view)
        mirrored = jnp.where(swap, flipped[VB - 1 - w], flipped[w])
        wall[w, :stacked] = combine(
            residuals[w][:stacked], mirrored[stacked:], red_own[:, span], ray_weight[:, span]
        )
        wall[w, stacked:] = combine(
            residuals[w][stacked:], mirrored[:stacked], red_part[:, span], part_weight[:, span]
        )
        wall_copy(w).start()
    for w in range(VB):
        back_copy(w).start()
        out_weighted(w).start()

    for p in range(frames // 2):
        taps = coefs[p * pair : (p + 1) * pair, :].astype(F32)
        for i in range(2):
            f = 2 * p + i
            masks = [columns[f] == float(j - HALO) for j in range(HALO + 1)]
            for m in range(2 * HALO + 1):
                value = None
                for k in range(max(0, m - HALO), min(TAPS, m + 1)):
                    start = (i * TAPS + k) * rows
                    term = jnp.where(masks[m - k], taps[start : start + rows], 0.0)
                    value = term if value is None else value + term
                omega[f, m] = value

    cuts = product.shape[0]
    width = sector // cuts

    def multiply():
        for t in range(count):
            total = None
            for w in range(VB):
                both = jnp.concatenate([wall[w], wall_in[w]], axis=0)
                cut = slice(w * view, (w + 1) * view)
                if t < turned.shape[0]:
                    value = jnp.dot(both, turned[t, cut, :], preferred_element_type=F32)
                else:
                    value = lax.dot_general(
                        both,
                        tiles[t, :, cut],
                        (((1,), (1,)), ((), ())),
                        preferred_element_type=F32,
                    )
                total = value if total is None else total + value
            for c in range(cuts):
                product[c, t] = total[:, c * width : (c + 1) * width]

    def partial(c, i, n):
        total = None
        for q in range(4):
            term = product[c, pick[2 * i + n, q], q * stacked : (q + 1) * stacked, :]
            total = term if total is None else total + term
        return total

    def sib_copy(c):
        return remote(sib_out.at[c], sib_in.at[c], sb_send.at[c], sb_recv.at[c], sibling)

    def far_copy(c, dh, dp):
        i = slot(dh, dp)
        return remote(
            far_out.at[c, i],
            far_in.at[c, i],
            fr_send.at[c, i - 1],
            fr_recv.at[c, i - 1],
            2 * chip_at(dh, dp) + 1 - core,
        )

    def give(c):
        for i, (dh, dp) in enumerate(everyone):
            sib_out[c, slot(dh, dp)] = partial(c, i, 0).astype(BF16)
        sib_copy(c).start()

    def pass_on(c):
        for n, (dh, dp) in enumerate(reversed(everyone)):
            i = slot(dh, dp)
            value = partial(c, everyone.index((dh, dp)), 1)
            if n == 0:
                sib_copy(c).wait_recv()
            value = value + sib_in[c, i].astype(F32)
            if (dh, dp) == (0, 0):
                image[half, :, c * width : (c + 1) * width] = value
            else:
                far_out[c, i] = value.astype(BF16)
                far_copy(c, dh, dp).start()

    def collect(c):
        span = slice(c * width, (c + 1) * width)
        same = image[half, :, span]
        other = None
        for dh, dp in others:
            far_copy(c, dh, dp).wait_recv()
            value = far_in[c, slot(dh, dp)].astype(F32)
            if dh:
                other = value if other is None else other + value
            else:
                same = same + value
        image[half, :, span] = same
        image[1 - half, :, span] = other

    for w in range(VB):
        wall_copy(w).wait_recv()
    multiply()
    for c in range(cuts):
        give(c)
    for c in range(cuts - 1):
        pass_on(c)
    pass_on(cuts - 1)

    totals = []
    for c in range(cuts):
        collect(c)
        span = slice(c * width, (c + 1) * width)
        spread = [None] * (2 * HALO + 1)
        for f in range(frames):
            g = f % (frames // 2)
            slices = image[f // (frames // 2), g * rows : (g + 1) * rows, span]
            for m in range(2 * HALO + 1):
                term = omega[f, m, :, span] * slices
                spread[m] = term if spread[m] is None else spread[m] + term
        total = None
        for m in range(2 * HALO + 1):
            pieces = [jnp.zeros((m, width), F32)] if m else []
            pieces.append(spread[m])
            if m < 2 * HALO:
                pieces.append(jnp.zeros((2 * HALO - m, width), F32))
            padded = jnp.concatenate(pieces, axis=0)
            total = padded if total is None else total + padded
        adj_out[0, :, span] = total[:HALO]
        adj_out[1, :, span] = total[rows + HALO :]
        totals.append(total[HALO : rows + HALO])
    exchange(adj_out, edges_hbm, ha_send, ha_recv)
    base[...] = vol + voxel_weight[...] * jnp.concatenate(totals, axis=1)
    out_base = pltpu.make_async_copy(base, base_hbm, out_sem.at[0])
    out_base.start()
    for j in range(2):
        for dh, dp in others:
            cross(dh, dp, j).wait_send()
        for dh, dp in everyone:
            to_sibling(dh, dp, j).wait_send()
    for copy in partner_copies:
        copy.wait_send()
    for w in range(VB):
        proj_copy(w).wait_send()
        wall_copy(w).wait_send()
        back_copy(w).wait()
        out_weighted(w).wait()
    for c in range(cuts):
        sib_copy(c).wait_send()
        for dh, dp in others:
            far_copy(c, dh, dp).wait_send()

    @pl.when(slab == 0)
    def _():
        pltpu.make_async_copy(zeros, edges_hbm.at[0], zero_sem.at[0]).wait()

    @pl.when(slab == slabs - 1)
    def _():
        pltpu.make_async_copy(zeros, edges_hbm.at[1], zero_sem.at[0]).wait()

    out_base.wait()
    exchange_wait(adj_out, edges_hbm, ha_send, ha_recv)


def settle(
    base_in,
    edges_in,
    scale_in,
    weighted_in,
    next_out,
    weighted_out,
    base,
    edges,
    scale,
    rows,
    in_sem,
    out_sem,
):
    loads = [
        pltpu.make_async_copy(src, dst, in_sem.at[n])
        for n, (src, dst) in enumerate(
            ((weighted_in, rows), (base_in, base), (edges_in, edges), (scale_in, scale))
        )
    ]
    for load in loads:
        load.start()
    out_rows = pltpu.make_async_copy(rows, weighted_out, out_sem.at[0])
    out_next = pltpu.make_async_copy(base, next_out, out_sem.at[1])
    loads[0].wait()
    out_rows.start()
    for load in loads[1:]:
        load.wait()
    middle = jnp.zeros((base.shape[0] - 2 * HALO, base.shape[1]), F32)
    adjoint = jnp.concatenate([edges[0], middle, edges[1]], axis=0)
    base[...] = base[...] + scale[...] * adjoint
    out_next.start()
    out_rows.wait()
    out_next.wait()


def body(
    volume,
    measured,
    tiles,
    tile_index,
    warp_coef,
    warp_offset,
    ray_weight,
    redundancy,
    conj_view,
    voxel_weight,
):
    frames, rows, rays = measured.shape
    sector = volume.shape[1]
    blocks = lax.axis_size("angle")
    slabs = lax.axis_size("frame")
    stacked = frames * rows
    chips = blocks // 2
    mine = tiles.shape[0] // 2
    view = rays // VB
    cuts = 2
    hbm = pl.BlockSpec(memory_space=pl.ANY)
    dma = pltpu.SemaphoreType.DMA
    flops = 4 * stacked * blocks * sector * rays
    base, edges, weighted = pl.pallas_call(
        functools.partial(kernel, blocks, slabs, frames, rows),
        out_shape=(
            jax.ShapeDtypeStruct(volume.shape, F32),
            jax.ShapeDtypeStruct((2, HALO, sector), F32),
            jax.ShapeDtypeStruct((stacked, rays), BF16),
        ),
        in_specs=[hbm] * 10,
        out_specs=(hbm, hbm, hbm),
        scratch_shapes=[
            pltpu.VMEM(volume.shape, F32),
            pltpu.VMEM((stacked // 2, rays), BF16),
            pltpu.VMEM((frames * TAPS * rows, sector), BF16),
            pltpu.VMEM(warp_offset.shape, jnp.int32),
            pltpu.VMEM(ray_weight.shape, F32),
            pltpu.VMEM((rays,), F32),
            pltpu.VMEM(voxel_weight.shape, F32),
            pltpu.SMEM(tile_index.shape, jnp.int32),
            pltpu.SMEM(conj_view.shape, jnp.int32),
            pltpu.SMEM((4, mine), jnp.int32),
            pltpu.SMEM((2 * chips, 4), jnp.int32),
            pltpu.VMEM(volume.shape, F32),
            pltpu.VMEM((HALO, sector), F32),
            pltpu.VMEM((frames, 2 * HALO + 1, rows, sector), F32),
            pltpu.VMEM((mine,) + tiles.shape[1:], BF16),
            pltpu.VMEM((3, rays, sector), BF16),
            pltpu.VMEM((blocks, 2, stacked // 4, sector), BF16),
            pltpu.VMEM((2, stacked // 4, sector), BF16),
            pltpu.VMEM((VB, stacked, view), F32),
            pltpu.VMEM((VB, stacked, view), F32),
            pltpu.VMEM((VB, stacked, view), F32),
            pltpu.VMEM((stacked // 2, rays), BF16),
            pltpu.VMEM(ray_weight.shape, F32),
            pltpu.VMEM((rays,), F32),
            pltpu.VMEM((VB, stacked, view), BF16),
            pltpu.VMEM((VB, stacked, view), BF16),
            pltpu.VMEM((cuts, mine + 1, 2 * stacked, sector // cuts), F32),
            pltpu.VMEM((2, stacked // 2, sector), F32),
            pltpu.VMEM((2, HALO, sector), F32),
            pltpu.VMEM((2, HALO, sector), F32),
            pltpu.VMEM((2, HALO, sector), F32),
            pltpu.VMEM((cuts, chips, stacked // 2, sector // cuts), BF16),
            pltpu.VMEM((cuts, chips, stacked // 2, sector // cuts), BF16),
            pltpu.VMEM((cuts, chips, stacked // 2, sector // cuts), BF16),
            pltpu.VMEM((cuts, chips, stacked // 2, sector // cuts), BF16),
            dma((9,)),
            dma((1 + VB,)),
            dma((1,)),
            dma((mine,)),
            dma((chips - 1, 2)),
            dma((chips - 1, 2)),
            dma((chips, 2)),
            dma((chips, 2)),
            dma((3,)),
            dma((3,)),
            dma((VB,)),
            dma((VB,)),
            dma((2, VB)),
            dma((2, VB)),
            dma((2,)),
            dma((2,)),
            dma((2,)),
            dma((2,)),
            dma((cuts,)),
            dma((cuts,)),
            dma((cuts, chips - 1)),
            dma((cuts, chips - 1)),
        ],
        cost_estimate=pl.CostEstimate(
            flops=flops, bytes_accessed=2 * tiles.size, transcendentals=0
        ),
        compiler_params=pltpu.CompilerParams(
            collective_id=0, has_side_effects=True, vmem_limit_bytes=62 * 1024 * 1024
        ),
    )(
        volume,
        measured.reshape(stacked, rays),
        tiles,
        tile_index,
        warp_coef.reshape(frames * TAPS * rows, sector),
        warp_offset,
        ray_weight,
        redundancy,
        conj_view,
        voxel_weight,
    )
    volume_next, weighted = pl.pallas_call(
        settle,
        out_shape=(
            jax.ShapeDtypeStruct(volume.shape, F32),
            jax.ShapeDtypeStruct((stacked, rays), BF16),
        ),
        in_specs=[hbm] * 4,
        out_specs=(hbm, hbm),
        scratch_shapes=[
            pltpu.VMEM(volume.shape, F32),
            pltpu.VMEM((2, HALO, sector), F32),
            pltpu.VMEM(volume.shape, F32),
            pltpu.VMEM((stacked, rays), BF16),
            dma((4,)),
            dma((2,)),
        ],
    )(base, edges, voxel_weight, weighted)
    return volume_next, weighted.reshape(frames, rows, rays)


def solution(mesh):
    placed = (
        P("frame", "angle"),
        P(None, "frame", "angle"),
        P(),
        P(),
        P(None, None, "frame", "angle"),
        P(None, "frame"),
        P("frame", "angle"),
        P("angle"),
        P("angle", None),
        P("frame", "angle"),
    )
    return jax.shard_map(
        body,
        mesh=mesh,
        in_specs=placed,
        out_specs=(P("frame", "angle"), P(None, "frame", "angle")),
        check_vma=False,
    )
```

```python
import functools

import jax
import jax.numpy as jnp
from jax import lax
from jax.experimental import pallas as pl
from jax.experimental.pallas import tpu as pltpu
from jax.sharding import PartitionSpec as P

VB = 2
HALO = 2
TAPS = 3
MESH = pl.DeviceIdType.MESH
F32 = jnp.float32
BF16 = jnp.bfloat16


def kernel(
    blocks,
    slabs,
    frames,
    rows,
    volume_hbm,
    measured_hbm,
    tiles_hbm,
    index_hbm,
    coefs_hbm,
    offsets_hbm,
    weight_hbm,
    red_hbm,
    conj_hbm,
    voxel_hbm,
    base_hbm,
    edges_hbm,
    weighted_hbm,
    volume,
    measured,
    coefs,
    offsets,
    ray_weight,
    redundancy,
    voxel_weight,
    tile_index,
    conj_view,
    find,
    pick,
    base,
    zeros,
    omega,
    tiles,
    turned,
    gathered,
    away,
    proj_mine,
    proj_out,
    proj_in,
    part_measured,
    part_weight,
    part_red,
    wall,
    wall_in,
    product,
    image,
    vol_out,
    vol_in,
    adj_out,
    sib_out,
    sib_in,
    far_out,
    far_in,
    in_sem,
    out_sem,
    zero_sem,
    tile_sem,
    ag_send,
    ag_recv,
    fw_send,
    fw_recv,
    pt_send,
    pt_recv,
    pj_send,
    pj_recv,
    wt_send,
    wt_recv,
    hv_send,
    hv_recv,
    ha_send,
    ha_recv,
    sb_send,
    sb_recv,
    fr_send,
    fr_recv,
):
    me = lax.axis_index("angle")
    slab = lax.axis_index("frame")
    chips = blocks // 2
    ring = chips // 2
    core = lax.rem(me, 2)
    chip = me // 2
    half = chip // ring
    place = lax.rem(chip, ring)
    sibling = me + 1 - 2 * core

    def chip_at(dh, dp):
        return lax.rem(half + dh, 2) * ring + lax.rem(place + dp, ring)

    def chip_from(dh, dp):
        return lax.rem(half + dh, 2) * ring + lax.rem(place + ring - dp, ring)

    partner = 2 * chip_at(1, 0) + core
    group = [me, partner, sibling, 2 * chip_at(1, 0) + 1 - core]
    others = [(dh, dp) for dp in range(ring) for dh in range(2) if dh or dp]
    everyone = [(0, 0)] + others
    count = tiles.shape[0]
    first = core * count
    stacked = frames * rows // 2
    sector = volume.shape[1]
    rays = measured.shape[1]
    view = rays // VB
    has_low = slab > 0
    has_high = slab < slabs - 1

    def remote(src, dst, send, recv, angle, frame=slab):
        return pltpu.make_async_remote_copy(
            src_ref=src,
            dst_ref=dst,
            send_sem=send,
            recv_sem=recv,
            device_id=(angle, frame),
            device_id_type=MESH,
        )

    def tile_copy(t):
        return pltpu.make_async_copy(tiles_hbm.at[first + t], tiles.at[t], tile_sem.at[t])

    barrier = pltpu.get_barrier_semaphore()
    pl.semaphore_signal(barrier, inc=1, device_id=(sibling, slab), device_id_type=MESH)
    for dh, dp in others:
        for other in (core, 1 - core):
            pl.semaphore_signal(
                barrier, inc=1, device_id=(2 * chip_at(dh, dp) + other, slab), device_id_type=MESH
            )

    @pl.when(has_low)
    def _():
        pl.semaphore_signal(barrier, inc=1, device_id=(me, slab - 1), device_id_type=MESH)

    @pl.when(has_high)
    def _():
        pl.semaphore_signal(barrier, inc=1, device_id=(me, slab + 1), device_id_type=MESH)

    measured_half = measured_hbm.at[pl.ds(pl.multiple_of(half * stacked, 16), stacked)]
    measured_away = measured_hbm.at[pl.ds(pl.multiple_of((1 - half) * stacked, 16), stacked)]
    local = [
        pltpu.make_async_copy(src, dst, in_sem.at[n])
        for n, (src, dst) in enumerate(
            (
                (volume_hbm, volume),
                (coefs_hbm, coefs),
                (offsets_hbm, offsets),
                (index_hbm, tile_index),
                (conj_hbm, conj_view),
                (measured_half, measured),
                (weight_hbm, ray_weight),
                (red_hbm, redundancy),
                (voxel_hbm, voxel_weight),
            )
        )
    ]
    for copy in local:
        copy.start()
    for t in range(count):
        tile_copy(t).start()
    local[0].wait()
    vol = volume[...]
    vol_out[0] = vol[:HALO]
    vol_out[1] = vol[rows - HALO :]

    peers = blocks - 1 + has_low.astype(jnp.int32) + has_high.astype(jnp.int32)
    pl.semaphore_wait(barrier, peers)

    def halo(out, into, send, recv, side):
        return remote(
            out.at[side], into.at[1 - side], send.at[side], recv.at[1 - side], me, slab + 2 * side - 1
        )

    def exchange(out, into, send, recv):
        @pl.when(has_low)
        def _():
            halo(out, into, send, recv, 0).start()

        @pl.when(has_high)
        def _():
            halo(out, into, send, recv, 1).start()

    def exchange_wait(out, into, send, recv):
        @pl.when(has_low)
        def _():
            halo(out, into, send, recv, 0).wait_send()
            halo(out, into, send, recv, 1).wait_recv()

        @pl.when(has_high)
        def _():
            halo(out, into, send, recv, 1).wait_send()
            halo(out, into, send, recv, 0).wait_recv()

    exchange(vol_out, vol_in, hv_send, hv_recv)
    local[1].wait()
    local[2].wait()

    off = offsets[...].astype(F32)
    lane = lax.broadcasted_iota(jnp.int32, (rows, rows), 1)
    diagonal = lane == lax.broadcasted_iota(jnp.int32, (rows, rows), 0)

    def offset_column(f):
        spread = jnp.broadcast_to(off[f : f + 1, :], (rows, rows))
        return jnp.sum(jnp.where(diagonal, spread, 0.0), axis=1, keepdims=True)

    columns = [offset_column(f) for f in range(frames)]
    pair = 2 * TAPS * rows

    def warp(below, above):
        extended = jnp.concatenate([below, vol, above], axis=0)
        sources = [extended[m : m + rows] for m in range(2 * HALO + 1)]
        warped = []
        for p in range(frames // 2):
            taps = coefs[p * pair : (p + 1) * pair, :].astype(F32)
            for i in range(2):
                column = columns[2 * p + i]
                low = column == -2.0
                mid = column == -1.0
                total = None
                for k in range(TAPS):
                    start = (i * TAPS + k) * rows
                    chosen = jnp.where(
                        low, sources[k], jnp.where(mid, sources[k + 1], sources[k + 2])
                    )
                    term = taps[start : start + rows] * chosen
                    total = term if total is None else total + term
                warped.append(total)
        return warped

    def keep(j, pieces):
        each = len(pieces) // 2
        early = jnp.concatenate(pieces[:each], axis=0)
        late = jnp.concatenate(pieces[each:], axis=0)
        gathered[me, j] = jnp.where(half == 0, early, late).astype(BF16)
        away[j] = jnp.where(half == 0, late, early).astype(BF16)

    def slot(dh, dp):
        return dh * ring + dp

    def cross(dh, dp, j):
        return remote(
            away.at[j] if dh else gathered.at[me, j],
            gathered.at[me, j],
            ag_send.at[slot(dh, dp) - 1, j],
            ag_recv.at[slot(dh, dp) - 1, j],
            2 * chip_at(dh, dp) + core,
        )

    def to_sibling(dh, dp, j):
        block = 2 * chip_from(dh, dp) + core
        return remote(
            gathered.at[block, j],
            gathered.at[block, j],
            fw_send.at[slot(dh, dp), j],
            fw_recv.at[slot(dh, dp), j],
            sibling,
        )

    def spread_chunk(j):
        for dh, dp in reversed(others):
            cross(dh, dp, j).start()
        to_sibling(0, 0, j).start()

    def pass_chunk(j):
        for dh, dp in others:
            cross(dh, dp, j).wait_recv()
            to_sibling(dh, dp, j).start()

    partner_copies = [
        remote(measured_away, part_measured, pt_send.at[0], pt_recv.at[0], partner),
        remote(weight_hbm, part_weight, pt_send.at[1], pt_recv.at[1], partner),
        remote(red_hbm, part_red, pt_send.at[2], pt_recv.at[2], partner),
    ]
    block = 128

    def turn(t):
        tile_copy(t).wait()

        def step(n, carry):
            span = pl.ds(pl.multiple_of(n * block, block), block)
            turned[t, :, span] = tiles[t, span, :].T
            return carry

        lax.fori_loop(0, sector // block, step, 0)

    outside = jnp.zeros((HALO, sector), F32)
    keep(0, [value[HALO : rows - HALO] for value in warp(outside, outside)])
    spread_chunk(0)
    turn(0)
    for copy in partner_copies[1:]:
        copy.start()
    exchange_wait(vol_out, vol_in, hv_send, hv_recv)

    @pl.when(slab == 0)
    def _():
        vol_in[0] = jnp.zeros_like(vol_in[0])
        zeros[...] = jnp.zeros_like(zeros)
        pltpu.make_async_copy(zeros, edges_hbm.at[0], zero_sem.at[0]).start()

    @pl.when(slab == slabs - 1)
    def _():
        vol_in[1] = jnp.zeros_like(vol_in[1])
        zeros[...] = jnp.zeros_like(zeros)
        pltpu.make_async_copy(zeros, edges_hbm.at[1], zero_sem.at[0]).start()

    outer = []
    for value in warp(vol_in[0], vol_in[1]):
        outer += [jnp.concatenate([value[:HALO], value[rows - HALO :]], axis=0)]
    keep(1, outer)
    spread_chunk(1)
    partner_copies[0].start()
    turn(1)

    local[3].wait()
    for q in range(4):
        row = [tile_index[group[q], s] for s in range(blocks)]
        for t in range(count):
            at = jnp.int32(0)
            for s in range(blocks):
                at = jnp.where(row[s] == first + t, s, at)
            find[q, t] = at
    for i, (dh, dp) in enumerate(everyone):
        for n in range(2):
            s = 2 * chip_at(dh, dp) + (core if bool(n) == (i == 0) else 1 - core)
            for q in range(4):
                t = tile_index[group[q], s] - first
                ours = jnp.logical_and(t >= 0, t < count)
                pick[2 * i + n, q] = jnp.where(ours, t, count)

    pass_chunk(0)
    turn(2)
    pass_chunk(1)
    for t in range(turned.shape[0], count):
        tile_copy(t).wait()
    for j in range(2):
        for dh, dp in everyone:
            to_sibling(dh, dp, j).wait_recv()

    def proj_copy(w):
        return remote(proj_out.at[w], proj_in.at[w], pj_send.at[w], pj_recv.at[w], sibling)

    for w in range(VB):
        total = None
        for t in range(count):
            left = jnp.concatenate(
                [gathered[find[q, t]].reshape(stacked, sector) for q in range(4)], axis=0
            )
            term = jnp.dot(
                left, tiles[t, :, w * view : (w + 1) * view], preferred_element_type=F32
            )
            total = term if total is None else total + term
        proj_mine[w] = total[: 2 * stacked]
        proj_out[w] = total[2 * stacked :]

    for w in range(VB):
        proj_copy(w).start()
    product[:, count] = jnp.zeros_like(product[:, count])
    for copy in local[4:]:
        copy.wait()
    for copy in partner_copies:
        copy.wait_recv()

    inside = rows - 2 * HALO
    chunk = frames * inside // 2

    def in_order(value, base):
        pieces = []
        for f in range(frames // 2):
            a = base + f * inside
            b = base + chunk + f * 2 * HALO
            pieces += [value[b : b + HALO], value[a : a + inside], value[b + HALO : b + 2 * HALO]]
        return jnp.concatenate(pieces, axis=0)

    wide = 256
    each = view // wide
    flip = lax.broadcasted_iota(jnp.int32, (wide, wide), 0) + lax.broadcasted_iota(
        jnp.int32, (wide, wide), 1
    )
    flip = jnp.where(flip == wide - 1, 1.0, 0.0).astype(BF16)
    swap = conj_view[0, 0] == 1
    residuals = []
    flipped = []
    for w in range(VB):
        span = slice(w * view, (w + 1) * view)
        proj_copy(w).wait_recv()
        value = proj_mine[w] + proj_in[w]
        value = jnp.concatenate(
            [
                measured[:, span].astype(F32) - in_order(value, 0),
                part_measured[:, span].astype(F32) - in_order(value, stacked),
            ],
            axis=0,
        )
        residuals.append(value)
        tall = jnp.concatenate(
            [value[:, u * wide : (u + 1) * wide] for u in reversed(range(each))], axis=0
        )
        high = tall.astype(BF16)
        rest = (tall - high.astype(F32)).astype(BF16)
        tall = jnp.dot(high, flip, preferred_element_type=F32) + jnp.dot(
            rest, flip, preferred_element_type=F32
        )
        flipped.append(
            jnp.concatenate(
                [tall[u * 2 * stacked : (u + 1) * 2 * stacked] for u in range(each)], axis=1
            )
        )

    def combine(residual, mirrored, red, weight):
        red = jnp.broadcast_to(red, residual.shape)
        value = red * residual + (1.0 - red) * mirrored
        return (value * jnp.concatenate([weight] * (frames // 2), axis=0)).astype(BF16)

    def wall_copy(w):
        return remote(wall.at[w], wall_in.at[w], wt_send.at[0, w], wt_recv.at[0, w], sibling)

    place_rows = pl.ds(pl.multiple_of(half * stacked, 16), stacked)

    def out_weighted(w):
        return pltpu.make_async_copy(
            wall.at[w, pl.ds(0, stacked)],
            weighted_hbm.at[place_rows, pl.ds(w * view, view)],
            out_sem.at[1 + w],
        )

    def back_copy(w):
        return remote(
            wall.at[w, pl.ds(stacked, stacked)],
            weighted_hbm.at[place_rows, pl.ds(w * view, view)],
            wt_send.at[1, w],
            wt_recv.at[1, w],
            partner,
        )

    red_own = redundancy[...][None, :]
    red_part = part_red[...][None, :]
    for w in range(VB):
        span = slice(w * view, (w + 1) * view)
        mirrored = jnp.where(swap, flipped[VB - 1 - w], flipped[w])
        wall[w, :stacked] = combine(
            residuals[w][:stacked], mirrored[stacked:], red_own[:, span], ray_weight[:, span]
        )
        wall[w, stacked:] = combine(
            residuals[w][stacked:], mirrored[:stacked], red_part[:, span], part_weight[:, span]
        )
        wall_copy(w).start()
    for w in range(VB):
        back_copy(w).start()
        out_weighted(w).start()

    for p in range(frames // 2):
        taps = coefs[p * pair : (p + 1) * pair, :].astype(F32)
        for i in range(2):
            f = 2 * p + i
            masks = [columns[f] == float(j - HALO) for j in range(HALO + 1)]
            for m in range(2 * HALO + 1):
                value = None
                for k in range(max(0, m - HALO), min(TAPS, m + 1)):
                    start = (i * TAPS + k) * rows
                    term = jnp.where(masks[m - k], taps[start : start + rows], 0.0)
                    value = term if value is None else value + term
                omega[f, m] = value

    cuts = product.shape[0]
    width = sector // cuts

    def multiply():
        for t in range(count):
            total = None
            for w in range(VB):
                both = jnp.concatenate([wall[w], wall_in[w]], axis=0)
                cut = slice(w * view, (w + 1) * view)
                if t < turned.shape[0]:
                    value = jnp.dot(both, turned[t, cut, :], preferred_element_type=F32)
                else:
                    value = lax.dot_general(
                        both,
                        tiles[t, :, cut],
                        (((1,), (1,)), ((), ())),
                        preferred_element_type=F32,
                    )
                total = value if total is None else total + value
            for c in range(cuts):
                product[c, t] = total[:, c * width : (c + 1) * width]

    def partial(c, i, n):
        total = None
        for q in range(4):
            term = product[c, pick[2 * i + n, q], q * stacked : (q + 1) * stacked, :]
            total = term if total is None else total + term
        return total

    def sib_copy(c):
        return remote(sib_out.at[c], sib_in.at[c], sb_send.at[c], sb_recv.at[c], sibling)

    def far_copy(c, dh, dp):
        i = slot(dh, dp)
        return remote(
            far_out.at[c, i],
            far_in.at[c, i],
            fr_send.at[c, i - 1],
            fr_recv.at[c, i - 1],
            2 * chip_at(dh, dp) + 1 - core,
        )

    def give(c):
        for i, (dh, dp) in enumerate(everyone):
            sib_out[c, slot(dh, dp)] = partial(c, i, 0).astype(BF16)
        sib_copy(c).start()

    def pass_on(c):
        for n, (dh, dp) in enumerate(reversed(everyone)):
            i = slot(dh, dp)
            value = partial(c, everyone.index((dh, dp)), 1)
            if n == 0:
                sib_copy(c).wait_recv()
            value = value + sib_in[c, i].astype(F32)
            if (dh, dp) == (0, 0):
                image[half, :, c * width : (c + 1) * width] = value
            else:
                far_out[c, i] = value.astype(BF16)
                far_copy(c, dh, dp).start()

    def collect(c):
        span = slice(c * width, (c + 1) * width)
        same = image[half, :, span]
        other = None
        for dh, dp in others:
            far_copy(c, dh, dp).wait_recv()
            value = far_in[c, slot(dh, dp)].astype(F32)
            if dh:
                other = value if other is None else other + value
            else:
                same = same + value
        image[half, :, span] = same
        image[1 - half, :, span] = other

    for w in range(VB):
        wall_copy(w).wait_recv()
    multiply()
    for c in range(cuts):
        give(c)
    for c in range(cuts - 1):
        pass_on(c)
    pass_on(cuts - 1)

    totals = []
    for c in range(cuts):
        collect(c)
        span = slice(c * width, (c + 1) * width)
        spread = [None] * (2 * HALO + 1)
        for f in range(frames):
            g = f % (frames // 2)
            slices = image[f // (frames // 2), g * rows : (g + 1) * rows, span]
            for m in range(2 * HALO + 1):
                term = omega[f, m, :, span] * slices
                spread[m] = term if spread[m] is None else spread[m] + term
        total = None
        for m in range(2 * HALO + 1):
            pieces = [jnp.zeros((m, width), F32)] if m else []
            pieces.append(spread[m])
            if m < 2 * HALO:
                pieces.append(jnp.zeros((2 * HALO - m, width), F32))
            padded = jnp.concatenate(pieces, axis=0)
            total = padded if total is None else total + padded
        adj_out[0, :, span] = total[:HALO]
        adj_out[1, :, span] = total[rows + HALO :]
        totals.append(total[HALO : rows + HALO])
    exchange(adj_out, edges_hbm, ha_send, ha_recv)
    base[...] = vol + voxel_weight[...] * jnp.concatenate(totals, axis=1)
    out_base = pltpu.make_async_copy(base, base_hbm, out_sem.at[0])
    out_base.start()
    for j in range(2):
        for dh, dp in others:
            cross(dh, dp, j).wait_send()
        for dh, dp in everyone:
            to_sibling(dh, dp, j).wait_send()
    for copy in partner_copies:
        copy.wait_send()
    for w in range(VB):
        proj_copy(w).wait_send()
        wall_copy(w).wait_send()
        back_copy(w).wait()
        out_weighted(w).wait()
    for c in range(cuts):
        sib_copy(c).wait_send()
        for dh, dp in others:
            far_copy(c, dh, dp).wait_send()

    @pl.when(slab == 0)
    def _():
        pltpu.make_async_copy(zeros, edges_hbm.at[0], zero_sem.at[0]).wait()

    @pl.when(slab == slabs - 1)
    def _():
        pltpu.make_async_copy(zeros, edges_hbm.at[1], zero_sem.at[0]).wait()

    out_base.wait()
    exchange_wait(adj_out, edges_hbm, ha_send, ha_recv)


def settle(
    base_in,
    edges_in,
    scale_in,
    weighted_in,
    next_out,
    weighted_out,
    base,
    edges,
    scale,
    rows,
    in_sem,
    out_sem,
):
    pieces = 4
    each = rows.shape[0] // pieces
    spans = [pl.ds(n * each, each) for n in range(pieces)]
    loads = [
        pltpu.make_async_copy(src, dst, in_sem.at[n])
        for n, (src, dst) in enumerate(
            [(base_in, base), (edges_in, edges), (scale_in, scale)]
            + [(weighted_in.at[span], rows.at[span]) for span in spans]
        )
    ]
    for load in loads:
        load.start()
    stores = [
        pltpu.make_async_copy(rows.at[span], weighted_out.at[span], out_sem.at[n])
        for n, span in enumerate(spans)
    ]
    out_next = pltpu.make_async_copy(base, next_out, out_sem.at[pieces])
    for load in loads[:3]:
        load.wait()
    middle = jnp.zeros((base.shape[0] - 2 * HALO, base.shape[1]), F32)
    adjoint = jnp.concatenate([edges[0], middle, edges[1]], axis=0)
    base[...] = base[...] + scale[...] * adjoint
    out_next.start()
    for load, store in zip(loads[3:], stores):
        load.wait()
        store.start()
    for store in stores:
        store.wait()
    out_next.wait()


def body(
    volume,
    measured,
    tiles,
    tile_index,
    warp_coef,
    warp_offset,
    ray_weight,
    redundancy,
    conj_view,
    voxel_weight,
):
    frames, rows, rays = measured.shape
    sector = volume.shape[1]
    blocks = lax.axis_size("angle")
    slabs = lax.axis_size("frame")
    stacked = frames * rows
    chips = blocks // 2
    mine = tiles.shape[0] // 2
    view = rays // VB
    cuts = 2
    hbm = pl.BlockSpec(memory_space=pl.ANY)
    dma = pltpu.SemaphoreType.DMA
    flops = 4 * stacked * blocks * sector * rays
    base, edges, weighted = pl.pallas_call(
        functools.partial(kernel, blocks, slabs, frames, rows),
        out_shape=(
            jax.ShapeDtypeStruct(volume.shape, F32),
            jax.ShapeDtypeStruct((2, HALO, sector), F32),
            jax.ShapeDtypeStruct((stacked, rays), BF16),
        ),
        in_specs=[hbm] * 10,
        out_specs=(hbm, hbm, hbm),
        scratch_shapes=[
            pltpu.VMEM(volume.shape, F32),
            pltpu.VMEM((stacked // 2, rays), BF16),
            pltpu.VMEM((frames * TAPS * rows, sector), BF16),
            pltpu.VMEM(warp_offset.shape, jnp.int32),
            pltpu.VMEM(ray_weight.shape, F32),
            pltpu.VMEM((rays,), F32),
            pltpu.VMEM(voxel_weight.shape, F32),
            pltpu.SMEM(tile_index.shape, jnp.int32),
            pltpu.SMEM(conj_view.shape, jnp.int32),
            pltpu.SMEM((4, mine), jnp.int32),
            pltpu.SMEM((2 * chips, 4), jnp.int32),
            pltpu.VMEM(volume.shape, F32),
            pltpu.VMEM((HALO, sector), F32),
            pltpu.VMEM((frames, 2 * HALO + 1, rows, sector), F32),
            pltpu.VMEM((mine,) + tiles.shape[1:], BF16),
            pltpu.VMEM((3, rays, sector), BF16),
            pltpu.VMEM((blocks, 2, stacked // 4, sector), BF16),
            pltpu.VMEM((2, stacked // 4, sector), BF16),
            pltpu.VMEM((VB, stacked, view), F32),
            pltpu.VMEM((VB, stacked, view), F32),
            pltpu.VMEM((VB, stacked, view), F32),
            pltpu.VMEM((stacked // 2, rays), BF16),
            pltpu.VMEM(ray_weight.shape, F32),
            pltpu.VMEM((rays,), F32),
            pltpu.VMEM((VB, stacked, view), BF16),
            pltpu.VMEM((VB, stacked, view), BF16),
            pltpu.VMEM((cuts, mine + 1, 2 * stacked, sector // cuts), F32),
            pltpu.VMEM((2, stacked // 2, sector), F32),
            pltpu.VMEM((2, HALO, sector), F32),
            pltpu.VMEM((2, HALO, sector), F32),
            pltpu.VMEM((2, HALO, sector), F32),
            pltpu.VMEM((cuts, chips, stacked // 2, sector // cuts), BF16),
            pltpu.VMEM((cuts, chips, stacked // 2, sector // cuts), BF16),
            pltpu.VMEM((cuts, chips, stacked // 2, sector // cuts), BF16),
            pltpu.VMEM((cuts, chips, stacked // 2, sector // cuts), BF16),
            dma((9,)),
            dma((1 + VB,)),
            dma((1,)),
            dma((mine,)),
            dma((chips - 1, 2)),
            dma((chips - 1, 2)),
            dma((chips, 2)),
            dma((chips, 2)),
            dma((3,)),
            dma((3,)),
            dma((VB,)),
            dma((VB,)),
            dma((2, VB)),
            dma((2, VB)),
            dma((2,)),
            dma((2,)),
            dma((2,)),
            dma((2,)),
            dma((cuts,)),
            dma((cuts,)),
            dma((cuts, chips - 1)),
            dma((cuts, chips - 1)),
        ],
        cost_estimate=pl.CostEstimate(
            flops=flops, bytes_accessed=2 * tiles.size, transcendentals=0
        ),
        compiler_params=pltpu.CompilerParams(
            collective_id=0, has_side_effects=True, vmem_limit_bytes=62 * 1024 * 1024
        ),
    )(
        volume,
        measured.reshape(stacked, rays),
        tiles,
        tile_index,
        warp_coef.reshape(frames * TAPS * rows, sector),
        warp_offset,
        ray_weight,
        redundancy,
        conj_view,
        voxel_weight,
    )
    volume_next, weighted = pl.pallas_call(
        settle,
        out_shape=(
            jax.ShapeDtypeStruct(volume.shape, F32),
            jax.ShapeDtypeStruct((stacked, rays), BF16),
        ),
        in_specs=[hbm] * 4,
        out_specs=(hbm, hbm),
        scratch_shapes=[
            pltpu.VMEM(volume.shape, F32),
            pltpu.VMEM((2, HALO, sector), F32),
            pltpu.VMEM(volume.shape, F32),
            pltpu.VMEM((stacked, rays), BF16),
            dma((7,)),
            dma((5,)),
        ],
    )(base, edges, voxel_weight, weighted)
    return volume_next, weighted.reshape(frames, rows, rays)


def solution(mesh):
    placed = (
        P("frame", "angle"),
        P(None, "frame", "angle"),
        P(),
        P(),
        P(None, None, "frame", "angle"),
        P(None, "frame"),
        P("frame", "angle"),
        P("angle"),
        P("angle", None),
        P("frame", "angle"),
    )
    return jax.shard_map(
        body,
        mesh=mesh,
        in_specs=placed,
        out_specs=(P("frame", "angle"), P(None, "frame", "angle")),
        check_vma=False,
    )
```
